32 devices in a mesh: dp: 2 (over x), ctx: 4 (over y, core), tensor: 4 (over z).
Axes of the slice: x: 2, y: 2, z: 4, core: 2. Of those that a mesh axis runs over, the one named last changes fastest.
Arguments:
- tokens: bfloat16 [32, 1024, 1024], P('dp', 'ctx'), may hold values from -6 to 6
- segment_ids: int32 [32, 1024], P('dp', 'ctx'), may hold values from 0 to 3, as said below
- norm1_gain: bfloat16 [1024], P(('dp', 'ctx')), may hold values from 0.5 to 1.5
- norm1_shift: bfloat16 [1024], P(('dp', 'ctx')), may hold values from -1.75 to 1.75
- w_query: bfloat16 [1024, 1024], P(('dp', 'ctx'), 'tensor'), may hold values from -0.1875 to 0.1875
- w_key: bfloat16 [1024, 1024], P(('dp', 'ctx'), 'tensor'), may hold values from -0.1875 to 0.1875
- w_value: bfloat16 [1024, 1024], P(('dp', 'ctx'), 'tensor'), may hold values from -0.1875 to 0.1875
- query_bias: bfloat16 [16, 64], P('tensor', ('dp', 'ctx')), may hold values from -1.75 to 1.75
- value_bias: bfloat16 [16, 64], P('tensor', ('dp', 'ctx')), may hold values from -1.75 to 1.75
- w_out: bfloat16 [1024, 1024], P('tensor', ('dp', 'ctx')), may hold values from -0.75 to 0.75
- out_bias: bfloat16 [1024], P(('dp', 'ctx')), may hold values from -1.75 to 1.75
- norm2_gain: bfloat16 [1024], P(('dp', 'ctx')), may hold values from 0.5 to 1.5
- norm2_shift: bfloat16 [1024], P(('dp', 'ctx')), may hold values from -1.75 to 1.75
- w_up: bfloat16 [1024, 4096], P(('dp', 'ctx'), 'tensor'), may hold values from -0.1875 to 0.1875
- up_bias: bfloat16 [16, 256], P('tensor', ('dp', 'ctx')), may hold values from -1.75 to 1.75
- w_down: bfloat16 [4096, 1024], P('tensor', ('dp', 'ctx')), may hold values from -0.1875 to 0.1875
- down_bias: bfloat16 [1024], P(('dp', 'ctx')), may hold values from -1.75 to 1.75
- out_grad: bfloat16 [32, 1024, 1024], P('dp', 'ctx'), may hold values from -6 to 6
Outputs:
- outputs: bfloat16 [32, 1024, 1024], P('dp', 'ctx')
- tokens_grad: bfloat16 [32, 1024, 1024], P('dp', 'ctx')
- norm1_gain_grad: float32 [1024], P(('dp', 'ctx'))
- norm1_shift_grad: float32 [1024], P(('dp', 'ctx'))
- w_query_grad: float32 [1024, 1024], P(('dp', 'ctx'), 'tensor')
- w_key_grad: float32 [1024, 1024], P(('dp', 'ctx'), 'tensor')
- w_value_grad: float32 [1024, 1024], P(('dp', 'ctx'), 'tensor')
- query_bias_grad: float32 [16, 64], P('tensor', ('dp', 'ctx'))
- value_bias_grad: float32 [16, 64], P('tensor', ('dp', 'ctx'))
- w_out_grad: float32 [1024, 1024], P('tensor', ('dp', 'ctx'))
- out_bias_grad: float32 [1024], P(('dp', 'ctx'))
- norm2_gain_grad: float32 [1024], P(('dp', 'ctx'))
- norm2_shift_grad: float32 [1024], P(('dp', 'ctx'))
- w_up_grad: float32 [1024, 4096], P(('dp', 'ctx'), 'tensor')
- up_bias_grad: float32 [16, 256], P('tensor', ('dp', 'ctx'))
- w_down_grad: float32 [4096, 1024], P('tensor', ('dp', 'ctx'))
- down_bias_grad: float32 [1024], P(('dp', 'ctx'))
The draws below stay inside these ranges and needn't reach their ends.
Inputs may be any that keep to these rules, and one draw needn't show every extreme that they name: `segment_ids`: ids start at 0 and never fall along a sequence. In each group of 16 sequences one (drawn) is a single document; every other sequence holds exactly four documents of 200 tokens or more each.
All inputs are finite; a program needn't handle non-finite values.
Results may differ from the reference program's by a relative error of at most 0.017.
Values may be sent and summed in bfloat16 or wider, within the bound.
A program may use at most 384 MiB of HBM per device.

```python
import math
import jax
import jax.numpy as jnp
from jax import lax

D = 1024
HEADS = 16
FF = 4096
LENGTH = 1024
DOC_MIN = 200
SEQS_DP = 16
HEAD_DIM = 64
SEQUENCES = 32


def draw_segment_ids(key, part):
    row_keys = jax.random.split(jax.random.fold_in(key, 11), SEQUENCES)

    def boundary(row_key):
        extra = jax.random.randint(row_key, (3,), 0, LENGTH - 4 * DOC_MIN + 1).astype(jnp.int32)
        extra = jnp.sort(extra)
        return (DOC_MIN * jnp.arange(1, 4, dtype=jnp.int32) + extra).astype(jnp.int32)
    cuts = jax.vmap(boundary)(row_keys)
    groups = SEQUENCES // SEQS_DP
    picked = jax.random.randint(jax.random.fold_in(key, 12), (groups,), 0, SEQS_DP)
    row_index = jnp.arange(SEQUENCES)
    single = row_index % SEQS_DP == picked[row_index // SEQS_DP]
    cuts = jnp.where(single[:, None], LENGTH, cuts)
    places = jnp.arange(LENGTH)
    return jnp.sum((places[None, :, None] >= cuts[:, None, :]).astype(jnp.int32), axis=-1).astype(jnp.int32)


def block_scale(stream_key, dims, cuts, low, high):
    level = 1.0
    for dim, parts in cuts:
        draws = jax.random.uniform(jax.random.fold_in(jax.random.fold_in(stream_key, 6), dim), (parts,), jnp.float32, low / len(cuts), high / len(cuts))
        level = level * jnp.repeat(jnp.exp(draws), dims[dim] // parts).reshape((-1,) + (1,) * (len(dims) - 1 - dim))
    return level


def centred(stream_key, dims, scale, bound, cuts=(), kind=jnp.bfloat16):
    drawn = scale * jax.random.normal(stream_key, dims, jnp.float32)
    if cuts:
        drawn = drawn * block_scale(stream_key, dims, cuts, -0.22, 0.18)
    return jnp.clip(drawn, -bound, bound).astype(kind)


def setup_inputs(seed: int = 0) -> dict:
    key_of = jax.random.split(jax.random.key(seed), 19)
    return {
        "tokens": centred(key_of[0], (SEQUENCES, LENGTH, D), 1.0, 6.0, ((0, 2), (1, 4))),
        "segment_ids": draw_segment_ids(jax.random.fold_in(key_of[18], 71), 0),
        "norm1_gain": jnp.clip(1.0 + 0.1 * jax.random.normal(key_of[2], (D,), jnp.float32), 0.5, 1.5).astype(jnp.bfloat16),
        "norm1_shift": centred(key_of[3], (D,), 0.3, 1.75, ((0, 8),)),
        "w_query": centred(key_of[4], (D, D), D ** -0.5, 0.1875, ((0, 8), (1, 4))),
        "w_key": centred(key_of[5], (D, D), D ** -0.5, 0.1875, ((0, 8), (1, 4))),
        "w_value": centred(key_of[6], (D, D), D ** -0.5, 0.1875, ((0, 8), (1, 4))),
        "query_bias": centred(key_of[7], (HEADS, HEAD_DIM), 0.3, 1.75, ((0, 4), (1, 8))),
        "value_bias": centred(key_of[8], (HEADS, HEAD_DIM), 0.3, 1.75, ((0, 4), (1, 8))),
        "w_out": centred(key_of[9], (D, D), (D // 16) ** -0.5, 0.75, ((0, 4), (1, 8))),
        "out_bias": centred(key_of[10], (D,), 0.3, 1.75, ((0, 8),)),
        "norm2_gain": jnp.clip(1.0 + 0.1 * jax.random.normal(key_of[11], (D,), jnp.float32), 0.5, 1.5).astype(jnp.bfloat16),
        "norm2_shift": centred(key_of[12], (D,), 0.3, 1.75, ((0, 8),)),
        "w_up": centred(key_of[13], (D, FF), D ** -0.5, 0.1875, ((0, 8), (1, 4))),
        "up_bias": centred(key_of[14], (HEADS, FF // HEADS), 0.3, 1.75, ((0, 4), (1, 8))),
        "w_down": centred(key_of[15], (FF, D), (FF // 4) ** -0.5, 0.1875, ((0, 4), (1, 8))),
        "down_bias": centred(key_of[16], (D,), 0.3, 1.75, ((0, 8),)),
        "out_grad": centred(key_of[17], (SEQUENCES, LENGTH, D), 1.0, 6.0, ((0, 2), (1, 4))),
    }


@jax.custom_vjp
def low(v):
    return lax.optimization_barrier(v.astype(jnp.bfloat16)).astype(jnp.float32)

@jax.custom_vjp
def low_back(v):
    return v

def low_keep(v):
    return (low(v), None)

def low_pass(kept, grad):
    return (grad,)

def back_keep(v):
    return (v, None)

def back_low(kept, grad):
    return (low(grad),)
low.defvjp(low_keep, low_pass)
low_back.defvjp(back_keep, back_low)
EPSILON = 1e-05
PRECISION = lax.Precision.HIGHEST

def layer_norm(values, gain, shift):
    centre = values - lax.optimization_barrier(jnp.mean(values, axis=-1, keepdims=True))
    spread = lax.optimization_barrier(jnp.mean(centre * centre, axis=-1, keepdims=True))
    return centre * lax.rsqrt(spread + EPSILON) * gain + shift

def gelu_tanh(values):
    return 0.5 * values * (1.0 + jnp.tanh(0.7978845608028654 * (values + 0.044715 * values * values * values)))

def linear(left, right):
    return jnp.dot(left, right, precision=PRECISION, preferred_element_type=jnp.float32)

def sequence_forward(params, inputs, segment):
    norm1_gain, norm1_shift, w_query, w_key, w_value, query_bias, value_bias, w_out, out_bias, norm2_gain, norm2_shift, w_up, up_bias, w_down, down_bias = params
    normed_one = low(layer_norm(inputs, norm1_gain, norm1_shift))
    queries = low(low_back(linear(normed_one, w_query) + query_bias.reshape(-1)))
    key_rows = low(low_back(linear(normed_one, w_key)))
    value_rows = low(low_back(linear(normed_one, w_value) + value_bias.reshape(-1)))
    query_heads = queries.reshape(LENGTH, HEADS, HEAD_DIM)
    key_heads = key_rows.reshape(LENGTH, HEADS, HEAD_DIM)
    value_heads = value_rows.reshape(LENGTH, HEADS, HEAD_DIM)
    raw_scores = jnp.einsum('qhd,khd->hqk', query_heads, key_heads, precision=PRECISION)
    places = jnp.arange(LENGTH)
    offsets = (places[None, :] - places[:, None]).astype(jnp.float32)
    slopes = jnp.exp2(-8.0 * jnp.arange(1, HEADS + 1).astype(jnp.float32) / HEADS)
    scores = raw_scores * (1.0 / math.sqrt(HEAD_DIM)) + slopes[:, None, None] * offsets[None]
    allowed = (places[None, :] <= places[:, None]) & (segment[None, :] == segment[:, None])
    scores = low_back(jnp.where(allowed[None], scores, -1e+30))
    highest = lax.optimization_barrier(jnp.max(scores, axis=-1, keepdims=True))
    exponent = jnp.exp(scores - highest)
    softmaxed = exponent / lax.optimization_barrier(jnp.sum(exponent, axis=-1, keepdims=True))
    mixed_heads = jnp.einsum('hqk,khd->qhd', low(softmaxed), value_heads, precision=PRECISION).reshape(LENGTH, D)
    mixed_heads = low(low_back(mixed_heads))
    residual = inputs + low_back(linear(mixed_heads, w_out)) + out_bias
    normed_two = low(layer_norm(residual, norm2_gain, norm2_shift))
    activated = low(gelu_tanh(low_back(linear(normed_two, w_up) + up_bias.reshape(-1))))
    return residual + linear(activated, w_down) + down_bias

def reference(tokens, segment_ids, norm1_gain, norm1_shift, w_query, w_key, w_value, query_bias, value_bias, w_out, out_bias, norm2_gain, norm2_shift, w_up, up_bias, w_down, down_bias, out_grad):
    params = (norm1_gain.astype(jnp.float32), norm1_shift.astype(jnp.float32), w_query.astype(jnp.float32), w_key.astype(jnp.float32), w_value.astype(jnp.float32), query_bias.astype(jnp.float32), value_bias.astype(jnp.float32), w_out.astype(jnp.float32), out_bias.astype(jnp.float32), norm2_gain.astype(jnp.float32), norm2_shift.astype(jnp.float32), w_up.astype(jnp.float32), up_bias.astype(jnp.float32), w_down.astype(jnp.float32), down_bias.astype(jnp.float32))
    inputs = tokens.astype(jnp.float32)
    stepper = jax.checkpoint(sequence_forward)

    def forward_all(weights, values):

        def advance(carried, sequence):
            return (carried, stepper(weights, sequence[0], sequence[1]))
        unused, results = lax.scan(advance, jnp.zeros((), jnp.float32), (values, segment_ids))
        return results
    results, pullback = jax.vjp(forward_all, params, inputs)
    param_grads, input_grad = pullback(out_grad.astype(jnp.float32))
    return (results.astype(jnp.bfloat16), input_grad.astype(jnp.bfloat16), param_grads[0], param_grads[1], param_grads[2], param_grads[3], param_grads[4], param_grads[5], param_grads[6], param_grads[7], param_grads[8], param_grads[9], param_grads[10], param_grads[11], param_grads[12], param_grads[13], param_grads[14])
```

```python
import functools
import math

import jax
import jax.numpy as jnp
from jax import lax
from jax.experimental import pallas as pl
from jax.experimental.pallas import tpu as pltpu
from jax.sharding import PartitionSpec as P

HEADS = 16
MICRO = 2
HEAD_DIM = 64


EPSILON = 1e-05


def layer_norm(values, gain, shift):
    centre = values - jnp.mean(values, axis=-1, keepdims=True)
    spread = jnp.mean(centre * centre, axis=-1, keepdims=True)
    return centre * lax.rsqrt(spread + EPSILON) * gain + shift


def gelu_tanh(values):
    return (
        0.5
        * values
        * (1.0 + jnp.tanh(0.7978845608028654 * (values + 0.044715 * values * values * values)))
    )


def matmul(left, right):
    return jnp.dot(left, right, preferred_element_type=jnp.float32)


def matmul_left(left, right):
    return lax.dot_general(
        left, right, (((0,), (0,)), ((), ())), preferred_element_type=jnp.float32
    )


def matmul_right(left, right):
    return lax.dot_general(
        left, right, (((1,), (1,)), ((), ())), preferred_element_type=jnp.float32
    )


def full_total(partial_value):
    return lax.psum(partial_value, "tensor")


def scores_of(query_heads, key_heads, query_seg, key_seg, slopes, query_first):
    query_count = query_heads.shape[1]
    key_count = key_heads.shape[1]
    head_width = query_heads.shape[3]
    raw_scores = jnp.einsum(
        "bqhd,bkhd->bhqk", query_heads, key_heads, preferred_element_type=jnp.float32
    )
    query_place = query_first + jnp.arange(query_count)
    key_place = jnp.arange(key_count)
    offsets = (key_place[None, :] - query_place[:, None]).astype(jnp.float32)
    scores = (
        raw_scores * (1.0 / math.sqrt(head_width))
        + slopes[None, :, None, None] * offsets[None, None]
    )
    causal = (key_place[None, :] <= query_place[:, None])[None, None]
    same_doc = query_seg[:, None, :, None] == key_seg[:, None, None, :]
    return jnp.where(causal & same_doc, scores, -1e30)


def shards(
    tokens,
    segment_ids,
    norm1_gain,
    norm1_shift,
    w_query,
    w_key,
    w_value,
    query_bias,
    value_bias,
    w_out,
    out_bias,
    norm2_gain,
    norm2_shift,
    w_up,
    up_bias,
    w_down,
    down_bias,
    out_grad,
):
    seqs_local, span_len, model_width = tokens.shape
    micro_seqs = seqs_local // MICRO
    row_count = micro_seqs * span_len
    heads_local = query_bias.shape[0]
    cols_local = heads_local * HEAD_DIM
    ff_local = w_up.shape[1]
    length_all = span_len * lax.axis_size("ctx")
    span_first = lax.axis_index("ctx") * span_len
    head_global = lax.axis_index("tensor") * heads_local + jnp.arange(heads_local)
    slopes = jnp.exp2(-8.0 * (head_global + 1).astype(jnp.float32) / HEADS)
    scale = 1.0 / math.sqrt(HEAD_DIM)
    grad_query = jnp.zeros((model_width, cols_local), jnp.float32)
    grad_key = jnp.zeros((model_width, cols_local), jnp.float32)
    grad_value = jnp.zeros((model_width, cols_local), jnp.float32)
    grad_qbias = jnp.zeros((heads_local, HEAD_DIM), jnp.float32)
    grad_vbias = jnp.zeros((heads_local, HEAD_DIM), jnp.float32)
    grad_wout = jnp.zeros((cols_local, model_width), jnp.float32)
    grad_small = jnp.zeros((6, model_width), jnp.float32)
    grad_up = jnp.zeros((model_width, ff_local), jnp.float32)
    grad_ubias = jnp.zeros((heads_local, ff_local // heads_local), jnp.float32)
    grad_down = jnp.zeros((ff_local, model_width), jnp.float32)
    outputs_list = []
    inputs_grad_list = []
    for micro_index in range(MICRO):
        first = micro_index * micro_seqs
        inputs = (
            tokens[first : first + micro_seqs].reshape(row_count, model_width).astype(jnp.float32)
        )
        query_seg = segment_ids[first : first + micro_seqs]
        cotangent = out_grad[first : first + micro_seqs].reshape(row_count, model_width)
        weights = (
            lax.all_gather(norm1_gain, ("dp", "ctx"), axis=0, tiled=True),
            lax.all_gather(norm1_shift, ("dp", "ctx"), axis=0, tiled=True),
            lax.all_gather(w_query, ("dp", "ctx"), axis=0, tiled=True),
            lax.all_gather(w_key, ("dp", "ctx"), axis=0, tiled=True),
            lax.all_gather(w_value, ("dp", "ctx"), axis=0, tiled=True),
            lax.all_gather(query_bias, ("dp", "ctx"), axis=1, tiled=True),
            lax.all_gather(value_bias, ("dp", "ctx"), axis=1, tiled=True),
            lax.all_gather(w_out, ("dp", "ctx"), axis=1, tiled=True),
            lax.all_gather(out_bias, ("dp", "ctx"), axis=0, tiled=True),
            lax.all_gather(norm2_gain, ("dp", "ctx"), axis=0, tiled=True),
            lax.all_gather(norm2_shift, ("dp", "ctx"), axis=0, tiled=True),
            lax.all_gather(w_up, ("dp", "ctx"), axis=0, tiled=True),
            lax.all_gather(up_bias, ("dp", "ctx"), axis=1, tiled=True),
            lax.all_gather(w_down, ("dp", "ctx"), axis=1, tiled=True),
            lax.all_gather(down_bias, ("dp", "ctx"), axis=0, tiled=True),
        )
        (
            gain_one,
            shift_one,
            full_query,
            full_key,
            full_value,
            bias_query,
            bias_value,
            full_out,
            bias_out,
            gain_two,
            shift_two,
            full_up,
            bias_up,
            full_down,
            bias_down,
        ) = weights
        gain_one = gain_one.astype(jnp.float32)
        shift_one = shift_one.astype(jnp.float32)
        gain_two = gain_two.astype(jnp.float32)
        shift_two = shift_two.astype(jnp.float32)
        bias_out = bias_out.astype(jnp.float32)
        bias_down = bias_down.astype(jnp.float32)
        normed_one = layer_norm(inputs, gain_one, shift_one).astype(jnp.bfloat16)
        queries = (
            matmul(normed_one, full_query) + bias_query.reshape(-1).astype(jnp.float32)
        ).astype(jnp.bfloat16)
        key_rows = matmul(normed_one, full_key).astype(jnp.bfloat16)
        value_rows = (
            matmul(normed_one, full_value) + bias_value.reshape(-1).astype(jnp.float32)
        ).astype(jnp.bfloat16)
        local_pairs = jnp.concatenate([key_rows, value_rows], axis=1).reshape(
            micro_seqs, span_len, 2 * cols_local
        )
        pairs_all, key_seg = (
            lax.all_gather(local_pairs, "ctx", axis=1, tiled=True),
            lax.all_gather(query_seg.astype(jnp.bfloat16), "ctx", axis=1, tiled=True),
        )
        key_seg = key_seg.astype(jnp.float32)
        query_segf = query_seg.astype(jnp.float32)
        key_heads = pairs_all[:, :, :cols_local].reshape(
            micro_seqs, length_all, heads_local, HEAD_DIM
        )
        value_heads = pairs_all[:, :, cols_local:].reshape(
            micro_seqs, length_all, heads_local, HEAD_DIM
        )
        query_heads = queries.reshape(micro_seqs, span_len, heads_local, HEAD_DIM)
        scores = scores_of(query_heads, key_heads, query_segf, key_seg, slopes, span_first)
        highest = jnp.max(scores, axis=-1, keepdims=True)
        exponent = jnp.exp(scores - highest)
        totals = jnp.sum(exponent, axis=-1, keepdims=True)
        softmaxed = exponent / totals
        log_total = highest + jnp.log(totals)
        mixed_heads = jnp.einsum(
            "bhqk,bkhd->bqhd",
            softmaxed.astype(jnp.bfloat16),
            value_heads,
            preferred_element_type=jnp.float32,
        )
        mixed_low = mixed_heads.reshape(row_count, cols_local).astype(jnp.bfloat16)
        attn_part = matmul(mixed_low, full_out)
        residual = inputs + full_total(attn_part) + bias_out
        normed_two = layer_norm(residual, gain_two, shift_two).astype(jnp.bfloat16)
        pre_act = matmul(normed_two, full_up) + bias_up.reshape(-1).astype(jnp.float32)
        activated = gelu_tanh(pre_act).astype(jnp.bfloat16)
        mlp_part = matmul(activated, full_down)
        result_rows = (residual + full_total(mlp_part) + bias_down).astype(jnp.bfloat16)
        outputs_list.append(result_rows.reshape(micro_seqs, span_len, model_width))
        weights_back = (
            lax.all_gather(norm1_gain, ("dp", "ctx"), axis=0, tiled=True),
            lax.all_gather(norm1_shift, ("dp", "ctx"), axis=0, tiled=True),
            lax.all_gather(w_query, ("dp", "ctx"), axis=0, tiled=True),
            lax.all_gather(w_key, ("dp", "ctx"), axis=0, tiled=True),
            lax.all_gather(w_value, ("dp", "ctx"), axis=0, tiled=True),
            lax.all_gather(query_bias, ("dp", "ctx"), axis=1, tiled=True),
            lax.all_gather(value_bias, ("dp", "ctx"), axis=1, tiled=True),
            lax.all_gather(w_out, ("dp", "ctx"), axis=1, tiled=True),
            lax.all_gather(out_bias, ("dp", "ctx"), axis=0, tiled=True),
            lax.all_gather(norm2_gain, ("dp", "ctx"), axis=0, tiled=True),
            lax.all_gather(norm2_shift, ("dp", "ctx"), axis=0, tiled=True),
            lax.all_gather(w_up, ("dp", "ctx"), axis=0, tiled=True),
            lax.all_gather(up_bias, ("dp", "ctx"), axis=1, tiled=True),
            lax.all_gather(w_down, ("dp", "ctx"), axis=1, tiled=True),
            lax.all_gather(down_bias, ("dp", "ctx"), axis=0, tiled=True),
        )
        back_query = weights_back[2]
        back_key = weights_back[3]
        back_value = weights_back[4]
        back_out = weights_back[7]
        back_up = weights_back[11]
        back_down = weights_back[13]
        gain_one = weights_back[0].astype(jnp.float32)
        shift_one = weights_back[1].astype(jnp.float32)
        gain_two = weights_back[9].astype(jnp.float32)
        shift_two = weights_back[10].astype(jnp.float32)
        act_grad = matmul_right(cotangent, back_down)
        unused, gelu_pull = jax.vjp(gelu_tanh, pre_act)
        pre_grad = gelu_pull(act_grad)[0].astype(jnp.bfloat16)
        grad_down = grad_down + matmul_left(activated, cotangent)
        grad_ubias = grad_ubias + jnp.sum(pre_grad.astype(jnp.float32), axis=0).reshape(
            heads_local, -1
        )
        grad_up = grad_up + matmul_left(normed_two, pre_grad)
        normed_two_back = matmul_right(pre_grad, back_up)
        unused, norm_pull = jax.vjp(layer_norm, residual, gain_two, shift_two)
        resid_grad, gain_two_grad, shift_two_grad = norm_pull(full_total(normed_two_back))
        cot_rows = cotangent.astype(jnp.float32)
        resid_grad = resid_grad + cot_rows
        attn_grad = resid_grad.astype(jnp.bfloat16)
        grad_wout = grad_wout + matmul_left(mixed_low, attn_grad)
        mixed_grad = matmul_right(attn_grad, back_out).astype(jnp.bfloat16)
        mixed_grad_heads = mixed_grad.reshape(micro_seqs, span_len, heads_local, HEAD_DIM)
        scores = scores_of(query_heads, key_heads, query_segf, key_seg, slopes, span_first)
        softmaxed = jnp.exp(scores - log_total)
        prob_grad = jnp.einsum(
            "bqhd,bkhd->bhqk", mixed_grad_heads, value_heads, preferred_element_type=jnp.float32
        )
        delta = jnp.sum(softmaxed * prob_grad, axis=-1, keepdims=True)
        score_grad = (softmaxed * (prob_grad - delta)).astype(jnp.bfloat16)
        query_grad = (
            jnp.einsum("bhqk,bkhd->bqhd", score_grad, key_heads, preferred_element_type=jnp.float32)
            * scale
        )
        query_low = query_grad.reshape(row_count, cols_local).astype(jnp.bfloat16)
        key_grad = (
            jnp.einsum(
                "bhqk,bqhd->bkhd", score_grad, query_heads, preferred_element_type=jnp.float32
            )
            * scale
        )
        value_grad = jnp.einsum(
            "bhqk,bqhd->bkhd",
            softmaxed.astype(jnp.bfloat16),
            mixed_grad_heads,
            preferred_element_type=jnp.float32,
        )
        pair_grad = jnp.concatenate(
            [
                key_grad.reshape(micro_seqs, length_all, cols_local),
                value_grad.reshape(micro_seqs, length_all, cols_local),
            ],
            axis=2,
        )
        pair_own = lax.psum_scatter(
            pair_grad.astype(jnp.bfloat16), "ctx", scatter_dimension=1, tiled=True
        ).astype(jnp.float32)
        key_low = pair_own[:, :, :cols_local].reshape(row_count, cols_local).astype(jnp.bfloat16)
        value_low = pair_own[:, :, cols_local:].reshape(row_count, cols_local).astype(jnp.bfloat16)
        grad_query = grad_query + matmul_left(normed_one, query_low)
        grad_key = grad_key + matmul_left(normed_one, key_low)
        grad_value = grad_value + matmul_left(normed_one, value_low)
        grad_qbias = grad_qbias + jnp.sum(query_low.astype(jnp.float32), axis=0).reshape(
            heads_local, HEAD_DIM
        )
        grad_vbias = grad_vbias + jnp.sum(value_low.astype(jnp.float32), axis=0).reshape(
            heads_local, HEAD_DIM
        )
        normed_one_back = (
            matmul_right(query_low, back_query)
            + matmul_right(key_low, back_key)
            + matmul_right(value_low, back_value)
        )
        unused, first_pull = jax.vjp(layer_norm, inputs, gain_one, shift_one)
        input_grad, gain_one_grad, shift_one_grad = first_pull(full_total(normed_one_back))
        input_grad = (input_grad + resid_grad).astype(jnp.bfloat16)
        inputs_grad_list.append(input_grad.reshape(micro_seqs, span_len, model_width))
        grad_small = grad_small + jnp.stack(
            [
                gain_one_grad,
                shift_one_grad,
                jnp.sum(resid_grad, axis=0),
                gain_two_grad,
                shift_two_grad,
                jnp.sum(cot_rows, axis=0),
            ],
            axis=0,
        )
    summed = (
        lax.psum_scatter(
            grad_query.astype(jnp.bfloat16), ("dp", "ctx"), scatter_dimension=0, tiled=True
        ).astype(jnp.float32),
        lax.psum_scatter(
            grad_key.astype(jnp.bfloat16), ("dp", "ctx"), scatter_dimension=0, tiled=True
        ).astype(jnp.float32),
        lax.psum_scatter(
            grad_value.astype(jnp.bfloat16), ("dp", "ctx"), scatter_dimension=0, tiled=True
        ).astype(jnp.float32),
        lax.psum_scatter(
            grad_qbias.astype(jnp.bfloat16), ("dp", "ctx"), scatter_dimension=1, tiled=True
        ).astype(jnp.float32),
        lax.psum_scatter(
            grad_vbias.astype(jnp.bfloat16), ("dp", "ctx"), scatter_dimension=1, tiled=True
        ).astype(jnp.float32),
        lax.psum_scatter(
            grad_wout.astype(jnp.bfloat16), ("dp", "ctx"), scatter_dimension=1, tiled=True
        ).astype(jnp.float32),
        lax.psum_scatter(
            grad_small.astype(jnp.bfloat16), ("dp", "ctx"), scatter_dimension=1, tiled=True
        ).astype(jnp.float32),
        lax.psum_scatter(
            grad_up.astype(jnp.bfloat16), ("dp", "ctx"), scatter_dimension=0, tiled=True
        ).astype(jnp.float32),
        lax.psum_scatter(
            grad_ubias.astype(jnp.bfloat16), ("dp", "ctx"), scatter_dimension=1, tiled=True
        ).astype(jnp.float32),
        lax.psum_scatter(
            grad_down.astype(jnp.bfloat16), ("dp", "ctx"), scatter_dimension=1, tiled=True
        ).astype(jnp.float32),
    )
    (
        sum_query,
        sum_key,
        sum_value,
        sum_qbias,
        sum_vbias,
        sum_wout,
        sum_small,
        sum_up,
        sum_ubias,
        sum_down,
    ) = summed
    return (
        jnp.concatenate(outputs_list, axis=0),
        jnp.concatenate(inputs_grad_list, axis=0),
        sum_small[0],
        sum_small[1],
        sum_query,
        sum_key,
        sum_value,
        sum_qbias,
        sum_vbias,
        sum_wout,
        sum_small[2],
        sum_small[3],
        sum_small[4],
        sum_up,
        sum_ubias,
        sum_down,
        sum_small[5],
    )


ALL = ("dp", "ctx", "tensor")
NORMAL = (((1,), (0,)), ((), ()))
ROWS = (((1,), (1,)), ((), ()))
COLS = (((0,), (0,)), ((), ()))
QUERY_BLOCK = 256


def dot(left, right, dims):
    return lax.dot_general(left, right, dims, preferred_element_type=jnp.float32)


def scores_turned(query, key, slope, first, seg_query, seg_key, causal_from):
    count, block = key.shape[0], query.shape[0]
    raw = dot(key, query, ROWS) * (1.0 / math.sqrt(HEAD_DIM))
    key_place = lax.broadcasted_iota(jnp.int32, (count, 1), 0)
    query_place = first + lax.broadcasted_iota(jnp.int32, (1, block), 1)
    scores = raw + slope * (key_place - query_place).astype(jnp.float32)
    allowed = (key_place <= query_place) & (seg_key == seg_query)
    return jnp.where(allowed, scores, -1e30)


def attend_kernel(heads, block, slope_ref, row_ref, col_ref, qkv_ref, o_ref, lse_ref):
    step = pl.program_id(1)
    length = qkv_ref.shape[0]
    width = heads * HEAD_DIM
    for head in range(heads):
        lo = head * HEAD_DIM
        slope = slope_ref[step * heads + head]
        for first in range(0, length, block):
            last = first + block
            query = qkv_ref[first:last, lo : lo + HEAD_DIM]
            key = qkv_ref[0:last, width + lo : width + lo + HEAD_DIM]
            value = qkv_ref[0:last, 2 * width + lo : 2 * width + lo + HEAD_DIM]
            scores = scores_turned(
                query, key, slope, first, row_ref[:, first:last], col_ref[0:last, :], first
            )
            highest = jnp.max(scores, axis=0, keepdims=True)
            exponent = jnp.exp(scores - highest)
            totals = jnp.sum(exponent, axis=0, keepdims=True)
            softmaxed = (exponent * (1.0 / totals)).astype(jnp.bfloat16)
            mixed = dot(softmaxed, value, COLS)
            o_ref[first:last, lo : lo + HEAD_DIM] = mixed.astype(jnp.bfloat16)
            lse_ref[head : head + 1, first:last] = highest + jnp.log(totals)


def attend_back_kernel(
    heads, block, slope_ref, row_ref, col_ref, qkv_ref, do_ref, lse_ref, grad_ref, dk_ref, dv_ref
):
    step = pl.program_id(1)
    length = qkv_ref.shape[0]
    width = heads * HEAD_DIM
    scale = 1.0 / math.sqrt(HEAD_DIM)
    for head in range(heads):
        lo = head * HEAD_DIM
        slope = slope_ref[step * heads + head]
        for first in reversed(range(0, length, block)):
            last = first + block
            query = qkv_ref[first:last, lo : lo + HEAD_DIM]
            key = qkv_ref[0:last, width + lo : width + lo + HEAD_DIM]
            value = qkv_ref[0:last, 2 * width + lo : 2 * width + lo + HEAD_DIM]
            mixed_grad = do_ref[first:last, lo : lo + HEAD_DIM]
            scores = scores_turned(
                query, key, slope, first, row_ref[:, first:last], col_ref[0:last, :], first
            )
            softmaxed = jnp.exp(scores - lse_ref[head : head + 1, first:last])
            prob_grad = dot(value, mixed_grad, ROWS)
            delta = jnp.sum(softmaxed * prob_grad, axis=0, keepdims=True)
            score_grad = (softmaxed * (prob_grad - delta)).astype(jnp.bfloat16)
            prob_low = softmaxed.astype(jnp.bfloat16)
            query_grad = dot(score_grad, key, COLS) * scale
            grad_ref[first:last, lo : lo + HEAD_DIM] = query_grad.astype(jnp.bfloat16)
            key_grad = dot(score_grad, query, NORMAL)
            value_grad = dot(prob_low, mixed_grad, NORMAL)
            if last == length:
                dk_ref[...] = key_grad
                dv_ref[...] = value_grad
            else:
                dk_ref[0:last, :] += key_grad
                dv_ref[0:last, :] += value_grad
        grad_ref[:, width + lo : width + lo + HEAD_DIM] = (dk_ref[...] * scale).astype(jnp.bfloat16)
        grad_ref[:, 2 * width + lo : 2 * width + lo + HEAD_DIM] = dv_ref[...].astype(jnp.bfloat16)


def attention_specs(seqs, length, groups, heads):
    width = heads * HEAD_DIM
    return (
        pl.BlockSpec(memory_space=pltpu.SMEM),
        pl.BlockSpec((None, 1, length), lambda s, t: (s, 0, 0)),
        pl.BlockSpec((None, length, 1), lambda s, t: (s, 0, 0)),
        pl.BlockSpec((None, length, 3 * width), lambda s, t: (s, 0, t)),
        pl.BlockSpec((None, length, width), lambda s, t: (s, 0, t)),
        pl.BlockSpec((None, None, heads, length), lambda s, t: (s, t, 0, 0)),
    )


def attend(slopes, seg_row, seg_col, qkv, groups, heads):
    seqs, length, _ = qkv.shape
    specs = attention_specs(seqs, length, groups, heads)
    block = math.gcd(length, QUERY_BLOCK)
    return pl.pallas_call(
        functools.partial(attend_kernel, heads, block),
        grid=(seqs, groups),
        in_specs=list(specs[:4]),
        out_specs=[specs[4], specs[5]],
        out_shape=[
            jax.ShapeDtypeStruct((seqs, length, groups * heads * HEAD_DIM), jnp.bfloat16),
            jax.ShapeDtypeStruct((seqs, groups, heads, length), jnp.float32),
        ],
        compiler_params=pltpu.CompilerParams(vmem_limit_bytes=40 * 2**20),
        name="attend",
    )(slopes, seg_row, seg_col, qkv)


def attend_back(slopes, seg_row, seg_col, qkv, mixed_grad, log_total, groups, heads):
    seqs, length, _ = qkv.shape
    specs = attention_specs(seqs, length, groups, heads)
    block = math.gcd(length, QUERY_BLOCK)
    return pl.pallas_call(
        functools.partial(attend_back_kernel, heads, block),
        grid=(seqs, groups),
        in_specs=list(specs),
        out_specs=specs[3],
        out_shape=jax.ShapeDtypeStruct(qkv.shape, jnp.bfloat16),
        scratch_shapes=[
            pltpu.VMEM((length, HEAD_DIM), jnp.float32),
            pltpu.VMEM((length, HEAD_DIM), jnp.float32),
        ],
        compiler_params=pltpu.CompilerParams(vmem_limit_bytes=40 * 2**20),
        name="attend_back",
    )(slopes, seg_row, seg_col, qkv, mixed_grad, log_total)


def core_params(mib=56):
    return pltpu.CompilerParams(vmem_limit_bytes=mib * 2**20)


def cost(flops, moved):
    return pl.CostEstimate(flops=int(flops), bytes_accessed=int(moved), transcendentals=0)


TILE = 256
WEIGHT_ROWS = 128
WIDE = 128


def norm_parts(values):
    centre = values - jnp.mean(values, axis=-1, keepdims=True)
    spread = jnp.mean(centre * centre, axis=-1, keepdims=True)
    scale = lax.rsqrt(spread + EPSILON)
    return centre * scale, scale


def norm_back(grad, normed, scale, gain):
    scaled = grad * gain
    mean_one = jnp.mean(scaled, axis=-1, keepdims=True)
    mean_two = jnp.mean(scaled * normed, axis=-1, keepdims=True)
    return scale * (scaled - mean_one - normed * mean_two)


def column_sum(values):
    return jnp.sum(values, axis=0, keepdims=True)


def flat(ref):
    block = ref[...]
    return block.reshape(-1, block.shape[-1])


def joined(refs):
    blocks = [ref[...] for ref in refs]
    return jnp.concatenate(blocks[:4], axis=0), jnp.concatenate(blocks[4:], axis=0)


def ff_blocks(which, depth, hidden):
    def spec(block):
        def index(z, order):
            return (order[block] * 4 + lax.bitwise_xor(z, order[12]), which, 0, 0)

        return pl.BlockSpec((None, None, depth, hidden), index)

    return [spec(block) for block in range(8)]


def prefetched(grid, in_specs, out_specs, scratch=()):
    return pltpu.PrefetchScalarGridSpec(
        num_scalar_prefetch=1,
        grid=grid,
        in_specs=in_specs,
        out_specs=out_specs,
        scratch_shapes=list(scratch),
    )


def into_hidden(rows, near, far):
    half = rows.shape[1] // 2
    return dot(rows[:, :half], near, NORMAL) + dot(rows[:, half:], far, NORMAL)


def order_kernel(order_ref, pieces_ref, out_ref):
    columns = out_ref.shape[1] // WIDE
    for block in range(columns):
        place = pl.multiple_of(order_ref[block] * WIDE, WIDE)
        out_ref[:, block * WIDE : (block + 1) * WIDE] = pieces_ref[:, pl.ds(place, WIDE)]


def order_pieces(order, pieces):
    count, span, model = pieces.shape
    return pl.pallas_call(
        order_kernel,
        grid_spec=pltpu.PrefetchScalarGridSpec(
            num_scalar_prefetch=1,
            grid=(count,),
            in_specs=[pl.BlockSpec((None, span, model), lambda p, order: (order[8 + p], 0, 0))],
            out_specs=pl.BlockSpec((span, model), lambda p, order: (p, 0)),
        ),
        out_shape=jax.ShapeDtypeStruct((count * span, model), pieces.dtype),
        compiler_params=core_params(32),
        cost_estimate=cost(0, 4 * pieces.size),
        name="order_pieces",
    )(order, pieces)


def place_kernel(order_ref, pieces_ref, out_ref):
    out_ref[...] = pieces_ref[...]


def place_slots(order, pieces):
    count, span, model = pieces.shape

    def index(z, j, order):
        return (z * 4 + order[8 + j], 0, 0)

    return pl.pallas_call(
        place_kernel,
        grid_spec=prefetched(
            (count // 4, 4),
            [pl.BlockSpec((None, span, model), index)],
            pl.BlockSpec((None, span, model), lambda z, j, order: (z * 4 + j, 0, 0)),
        ),
        out_shape=jax.ShapeDtypeStruct(pieces.shape, pieces.dtype),
        compiler_params=core_params(32),
        cost_estimate=cost(0, 4 * pieces.size),
        name="place_slots",
    )(order, pieces)


MESH = pl.DeviceIdType.MESH


def partner(place, bits):
    if bits == 3:
        return 3 - place
    return place + bits - 2 * bits * lax.rem(lax.div(place, bits), 2)


def gather_kernel(
    cut,
    pack_ref,
    tokens_ref,
    seg_ref,
    out_ref,
    far_ref,
    pieces_ref,
    segs_ref,
    local_sems,
    ctx_send,
    ctx_recv,
    z_send,
    z_recv,
    hop_send,
    hop_recv,
):
    at_x = lax.axis_index("dp")
    at_ctx = lax.axis_index("ctx")
    at_z = lax.axis_index("tensor")
    ctx_of = [{"ctx": partner(at_ctx, bits)} for bits in (1, 2, 3)]
    z_of = [{"tensor": partner(at_z, bits)} for bits in (1, 2, 3)]
    x_of, y_of, core_of = {"dp": 1 - at_x}, ctx_of[1], ctx_of[0]

    barrier = pltpu.get_barrier_semaphore()
    for device in ctx_of + z_of + [x_of]:
        pl.semaphore_signal(barrier, inc=1, device_id=device, device_id_type=MESH)
    pl.semaphore_wait(barrier, 7)

    def remote(source, target, send, recv, device):
        copy = pltpu.make_async_remote_copy(
            src_ref=source,
            dst_ref=target,
            send_sem=send,
            recv_sem=recv,
            device_id=device,
            device_id_type=MESH,
        )
        copy.start()
        return copy

    def hop(stage, z, source, target, device):
        return remote(source, target, hop_send.at[stage, z], hop_recv.at[stage, z], device)

    def slot(bits):
        place = at_ctx if bits == 0 else partner(at_ctx, bits)
        return at_z * 4 + place

    local = [
        pltpu.make_async_copy(pack_ref, out_ref.at[0, 0, 0], local_sems.at[0]),
        pltpu.make_async_copy(tokens_ref.at[slot(0)], pieces_ref.at[0], local_sems.at[1]),
        pltpu.make_async_copy(seg_ref.at[slot(0)], segs_ref.at[0], local_sems.at[2]),
    ]
    for copy in local:
        copy.start()
    across = [
        remote(pack_ref, out_ref.at[0, 0, bits], z_send.at[bits], z_recv.at[bits], z_of[bits - 1])
        for bits in (1, 2, 3)
    ]

    def first_hops(z, source):
        return (
            hop(0, z, source.at[:cut], out_ref.at[0, 1, z, :cut], x_of),
            hop(1, z, source.at[cut:], out_ref.at[1, 0, z, cut:], y_of),
        )

    first = [first_hops(0, pack_ref)]
    others = []
    for bits in (1, 2, 3):
        device = ctx_of[bits - 1]
        for kind, (source, target) in enumerate(((tokens_ref, pieces_ref), (seg_ref, segs_ref))):
            send, recv = ctx_send.at[kind, bits], ctx_recv.at[kind, bits]
            others.append(remote(source.at[slot(bits)], target.at[bits], send, recv, device))
    for z in (1, 2, 3):
        across[z - 1].wait_recv()
        first.append(first_hops(z, out_ref.at[0, 0, z]))
    local[0].wait()
    second = []
    for z in range(4):
        first[z][0].wait_recv()
        source = out_ref.at[0, :, z, :cut]
        to_y = hop(2, z, source, out_ref.at[1, :, z, :cut], y_of)
        first[z][1].wait_recv()
        source = out_ref.at[:, 0, z, cut:]
        second.append((to_y, hop(3, z, source, out_ref.at[:, 1, z, cut:], x_of)))
    third = []
    for z in range(4):
        for copy in second[z]:
            copy.wait_recv()
        third.append(hop(4, z, out_ref.at[:, :, z], far_ref.at[:, :, z], core_of))
    for copy in third + others:
        copy.wait_recv()
    for copy in across + others + third:
        copy.wait_send()
    for pair in first + second:
        for copy in pair:
            copy.wait_send()
    local[1].wait()
    local[2].wait()


def gather_first(pack, tokens, segs, cut):
    rows, columns = pack.shape
    span, model = tokens.shape[1:]
    anywhere = pl.BlockSpec(memory_space=pl.ANY)
    sems = pltpu.SemaphoreType.DMA
    return pl.pallas_call(
        functools.partial(gather_kernel, cut),
        in_specs=[anywhere] * 3,
        out_specs=[anywhere] * 4,
        out_shape=[
            jax.ShapeDtypeStruct((2, 2, 4, rows, columns), pack.dtype),
            jax.ShapeDtypeStruct((2, 2, 4, rows, columns), pack.dtype),
            jax.ShapeDtypeStruct((4, span, model), tokens.dtype),
            jax.ShapeDtypeStruct((4,) + segs.shape[1:], segs.dtype),
        ],
        scratch_shapes=[
            sems((3,)),
            sems((2, 4)),
            sems((2, 4)),
            sems((4,)),
            sems((4,)),
            sems((5, 4)),
            sems((5, 4)),
        ],
        compiler_params=pltpu.CompilerParams(collective_id=0, has_side_effects=True),
        cost_estimate=cost(0, 128 * 2**20),
        name="gather_first",
    )(pack, tokens, segs)


def whole(*shape):
    zeros = (0,) * len(shape)
    return pl.BlockSpec(shape, lambda *_: zeros)


def weight_block(rows, columns, index):
    return pl.BlockSpec((4, None, rows, columns), lambda z: (0, z, 0, index))


def project_kernel(x_ref, gain_ref, shift_ref, bias_ref, near_ref, far_ref, h_ref, out_ref):
    rows = x_ref.shape[0]

    @pl.when(pl.program_id(0) == 0)
    def _():
        for first in range(0, rows, TILE):
            normed, _ = norm_parts(x_ref[first : first + TILE].astype(jnp.float32))
            h_ref[first : first + TILE] = (normed * gain_ref[...] + shift_ref[...]).astype(
                jnp.bfloat16
            )

    near, far = flat(near_ref), flat(far_ref)
    for first in range(0, rows, TILE):
        sums = into_hidden(h_ref[first : first + TILE], near, far) + bias_ref[...]
        out_ref[first : first + TILE] = sums.astype(jnp.bfloat16)


def project(x, gain, shift, bias, near, far, width):
    rows, model = x.shape
    groups = near.shape[1]
    return pl.pallas_call(
        project_kernel,
        grid=(groups,),
        in_specs=[
            whole(rows, model),
            whole(1, model),
            whole(1, model),
            pl.BlockSpec((None, 1, width), lambda z: (z, 0, 0)),
            weight_block(WEIGHT_ROWS, width, 0),
            weight_block(WEIGHT_ROWS, width, 0),
        ],
        out_specs=[whole(rows, model), pl.BlockSpec((rows, width), lambda z: (0, z))],
        out_shape=[
            jax.ShapeDtypeStruct((rows, model), jnp.bfloat16),
            jax.ShapeDtypeStruct((rows, groups * width), jnp.bfloat16),
        ],
        compiler_params=core_params(),
        cost_estimate=cost(2 * rows * model * groups * width, 2 * model * groups * width),
        name="project",
    )(x, gain, shift, bias, near, far)


def mix_out_kernel(
    o_ref, x_ref, bias_ref, gain_ref, shift_ref, near_ref, far_ref, x1_ref, h_ref
):
    groups, width = near_ref.shape[1], near_ref.shape[3]
    halves = []
    for weights in (near_ref, far_ref):
        total = None
        for z in range(groups):
            block = weights[:, z].reshape(-1, width)
            part = dot(o_ref[:, z * width : (z + 1) * width], block, ROWS)
            total = part if total is None else total + part
        halves.append(total)
    residual = x_ref[...].astype(jnp.float32) + jnp.concatenate(halves, axis=1) + bias_ref[...]
    x1_ref[...] = residual
    normed, _ = norm_parts(residual)
    h_ref[...] = (normed * gain_ref[...] + shift_ref[...]).astype(jnp.bfloat16)


def mix_out(o, x, bias, gain, shift, near, far, width):
    rows, model = x.shape
    groups = near.shape[1]
    rowed = pl.BlockSpec((TILE, model), lambda r: (r, 0))
    weights = pl.BlockSpec((4, groups, WEIGHT_ROWS, width), lambda r: (0, 0, 0, 3))
    return pl.pallas_call(
        mix_out_kernel,
        grid=(rows // TILE,),
        in_specs=[rowed, rowed, whole(1, model), whole(1, model), whole(1, model)] + [weights] * 2,
        out_specs=[rowed, rowed],
        out_shape=[
            jax.ShapeDtypeStruct((rows, model), jnp.float32),
            jax.ShapeDtypeStruct((rows, model), jnp.bfloat16),
        ],
        compiler_params=core_params(),
        cost_estimate=cost(2 * rows * model * model, 12 * rows * model),
        name="mix_out",
    )(o, x, bias, gain, shift, near, far)


def expand_kernel(order_ref, h_ref, bias_ref, *refs):
    near, far = joined(refs[:8])
    g_ref, slope_ref = refs[8:]
    root = 0.7978845608028654
    for first in range(0, h_ref.shape[0], TILE):
        a = into_hidden(h_ref[first : first + TILE], near, far) + bias_ref[...]
        square = a * a
        bent = jnp.tanh(a * (root + (root * 0.044715) * square))
        half = 0.5 * a
        g_ref[first : first + TILE] = (half + half * bent).astype(jnp.bfloat16)
        inner = root + (3.0 * root * 0.044715) * square
        slope_ref[first : first + TILE] = (
            0.5 + 0.5 * bent + half * (1.0 - bent * bent) * inner
        ).astype(jnp.bfloat16)


def expand(order, h, bias, weights):
    rows, model = h.shape
    depth, hidden = weights.shape[2:]
    groups = bias.shape[0]
    out = pl.BlockSpec((rows, hidden), lambda z, order: (0, z))
    return pl.pallas_call(
        expand_kernel,
        grid_spec=prefetched(
            (groups,),
            [whole(rows, model), pl.BlockSpec((None, 1, hidden), lambda z, order: (z, 0, 0))]
            + ff_blocks(0, depth, hidden),
            [out, out],
        ),
        out_shape=[jax.ShapeDtypeStruct((rows, groups * hidden), jnp.bfloat16)] * 2,
        compiler_params=core_params(),
        cost_estimate=cost(2 * rows * model * groups * hidden, 8 * rows * groups * hidden),
        name="expand",
    )(order, h, bias, *[weights] * 8)


def contract_kernel(order_ref, g_ref, x1_ref, bias_ref, *refs):
    step = pl.program_id(0)
    near, far = joined(refs[:8])
    out_ref, total_ref = refs[8:]
    rows, model = total_ref.shape
    half = model // 2

    @pl.when(step == 0)
    def _():
        total_ref[...] = x1_ref[...] + bias_ref[...]

    for first in range(0, rows, TILE):
        part = g_ref[first : first + TILE]
        total_ref[first : first + TILE, :half] += dot(part, near, ROWS)
        total_ref[first : first + TILE, half:] += dot(part, far, ROWS)

    @pl.when(step == pl.num_programs(0) - 1)
    def _():
        store_absolute(order_ref, total_ref, out_ref)


def store_absolute(order_ref, value_ref, out_ref):
    span = out_ref.shape[1]
    for piece in range(out_ref.shape[0]):
        for block in range(out_ref.shape[2] // WIDE):
            place = pl.multiple_of(order_ref[block] * WIDE, WIDE)
            out_ref[order_ref[8 + piece], :, pl.ds(place, WIDE)] = value_ref[
                piece * span : (piece + 1) * span, block * WIDE : (block + 1) * WIDE
            ].astype(out_ref.dtype)


def contract(order, g, x1, bias, weights, groups):
    rows, model = x1.shape
    depth, hidden = weights.shape[2:]
    return pl.pallas_call(
        contract_kernel,
        grid_spec=prefetched(
            (groups,),
            [
                pl.BlockSpec((rows, hidden), lambda z, order: (0, z)),
                whole(rows, model),
                whole(1, model),
            ]
            + ff_blocks(1, depth, hidden),
            whole(4, rows // 4, model),
            [pltpu.VMEM((rows, model), jnp.float32)],
        ),
        out_shape=jax.ShapeDtypeStruct((4, rows // 4, model), jnp.bfloat16),
        compiler_params=core_params(),
        cost_estimate=cost(2 * rows * model * groups * hidden, 4 * rows * groups * hidden),
        name="contract",
    )(order, g, x1, bias, *[weights] * 8)


def ff_back_kernel(order_ref, dy_ref, slope_ref, x1_ref, gain_ref, *refs):
    step = pl.program_id(0)
    near, far = joined(refs[:8])
    up_one, up_two = joined(refs[8:16])
    da_ref, ubias_ref, dx1_ref, dattn_ref, sums_ref, total_ref = refs[16:]
    rows, model = total_ref.shape
    half = model // 2

    @pl.when(step == 0)
    def _():
        total_ref[...] = jnp.zeros_like(total_ref)

    sums = None
    for first in range(0, rows, TILE):
        span = slice(first, first + TILE)
        da = into_hidden(dy_ref[span], near, far) * slope_ref[span].astype(jnp.float32)
        da = da.astype(jnp.bfloat16)
        da_ref[span] = da
        part = column_sum(da.astype(jnp.float32))
        sums = part if sums is None else sums + part
        total_ref[span, :half] += dot(da, up_one, ROWS)
        total_ref[span, half:] += dot(da, up_two, ROWS)
    ubias_ref[...] = sums

    @pl.when(step == pl.num_programs(0) - 1)
    def _():
        gains = shifts = outs = downs = jnp.zeros((1, model), jnp.float32)
        for first in range(0, rows, TILE):
            span = slice(first, first + TILE)
            normed, scale = norm_parts(x1_ref[span])
            grad = total_ref[span]
            dy = dy_ref[span].astype(jnp.float32)
            gains = gains + column_sum(grad * normed)
            shifts = shifts + column_sum(grad)
            downs = downs + column_sum(dy)
            dx1 = dy + norm_back(grad, normed, scale, gain_ref[...])
            outs = outs + column_sum(dx1)
            dx1_ref[span] = dx1
            dattn_ref[span] = dx1.astype(jnp.bfloat16)
        sums_ref[...] = jnp.concatenate([outs, gains, shifts, downs], axis=0)


def ff_back(order, dy, slope, x1, gain, weights, groups):
    rows, model = x1.shape
    depth, hidden = weights.shape[2:]
    column = pl.BlockSpec((rows, hidden), lambda z, order: (0, z))
    return pl.pallas_call(
        ff_back_kernel,
        grid_spec=prefetched(
            (groups,),
            [whole(rows, model), column, whole(rows, model), whole(1, model)]
            + ff_blocks(1, depth, hidden)
            + ff_blocks(0, depth, hidden),
            [
                column,
                pl.BlockSpec((None, 1, hidden), lambda z, order: (z, 0, 0)),
                whole(rows, model),
                whole(rows, model),
                whole(4, model),
            ],
            [pltpu.VMEM((rows, model), jnp.float32)],
        ),
        out_shape=[
            jax.ShapeDtypeStruct((rows, groups * hidden), jnp.bfloat16),
            jax.ShapeDtypeStruct((groups, 1, hidden), jnp.float32),
            jax.ShapeDtypeStruct((rows, model), jnp.float32),
            jax.ShapeDtypeStruct((rows, model), jnp.bfloat16),
            jax.ShapeDtypeStruct((4, model), jnp.float32),
        ],
        compiler_params=core_params(60),
        cost_estimate=cost(4 * rows * model * groups * hidden, 8 * rows * groups * hidden),
        name="ff_back",
    )(order, dy, slope, x1, gain, *[weights] * 16)


def mix_back_kernel(dattn_ref, near_ref, far_ref, out_ref):
    near, far = flat(near_ref), flat(far_ref)
    out_ref[...] = into_hidden(dattn_ref[...], near, far).astype(jnp.bfloat16)


def mix_back(dattn, near, far, width):
    rows, model = dattn.shape
    groups = near.shape[1]
    return pl.pallas_call(
        mix_back_kernel,
        grid=(groups,),
        in_specs=[whole(rows, model)] + [weight_block(WEIGHT_ROWS, width, 3)] * 2,
        out_specs=pl.BlockSpec((rows, width), lambda z: (0, z)),
        out_shape=jax.ShapeDtypeStruct((rows, groups * width), jnp.bfloat16),
        compiler_params=core_params(),
        cost_estimate=cost(2 * rows * model * groups * width, 6 * rows * model),
        name="mix_back",
    )(dattn, near, far)


def project_back_kernel(
    order_ref,
    grad_ref,
    x_ref,
    dx1_ref,
    gain_ref,
    near_ref,
    far_ref,
    out_ref,
    bias_ref,
    sums_ref,
    total_ref,
):
    step = pl.program_id(0)
    rows, model = total_ref.shape
    half = model // 2
    near, far = flat(near_ref), flat(far_ref)

    @pl.when(step == 0)
    def _():
        total_ref[...] = jnp.zeros_like(total_ref)

    sums = None
    for first in range(0, rows, TILE):
        span = slice(first, first + TILE)
        grad = grad_ref[span]
        part = column_sum(grad.astype(jnp.float32))
        sums = part if sums is None else sums + part
        total_ref[span, :half] += dot(grad, near, ROWS)
        total_ref[span, half:] += dot(grad, far, ROWS)
    bias_ref[...] = sums

    @pl.when(step == pl.num_programs(0) - 1)
    def _():
        gains = shifts = jnp.zeros((1, model), jnp.float32)
        for first in range(0, rows, TILE):
            span = slice(first, first + TILE)
            normed, scale = norm_parts(x_ref[span].astype(jnp.float32))
            grad = total_ref[span]
            gains = gains + column_sum(grad * normed)
            shifts = shifts + column_sum(grad)
            total_ref[span] = dx1_ref[span] + norm_back(grad, normed, scale, gain_ref[...])
        sums_ref[...] = jnp.concatenate([gains, shifts], axis=0)
        store_absolute(order_ref, total_ref, out_ref)


def project_back(order, grad, x, dx1, gain, near, far, width):
    rows, model = x.shape
    groups = near.shape[1]
    return pl.pallas_call(
        project_back_kernel,
        grid=(groups,),
        in_specs=[
            pl.BlockSpec(memory_space=pltpu.SMEM),
            pl.BlockSpec((rows, width), lambda z: (0, z)),
            whole(rows, model),
            whole(rows, model),
            whole(1, model),
            weight_block(WEIGHT_ROWS, width, 0),
            weight_block(WEIGHT_ROWS, width, 0),
        ],
        out_specs=[
            whole(4, rows // 4, model),
            pl.BlockSpec((None, 1, width), lambda z: (z, 0, 0)),
            whole(2, model),
        ],
        out_shape=[
            jax.ShapeDtypeStruct((4, rows // 4, model), jnp.bfloat16),
            jax.ShapeDtypeStruct((groups, 1, width), jnp.float32),
            jax.ShapeDtypeStruct((2, model), jnp.float32),
        ],
        scratch_shapes=[pltpu.VMEM((rows, model), jnp.float32)],
        compiler_params=core_params(),
        cost_estimate=cost(2 * rows * model * groups * width, 8 * rows * model),
        name="project_back",
    )(order, grad, x, dx1, gain, near, far)


def swap(value, axis, bits):
    count = lax.axis_size(axis)
    return lax.ppermute(value, axis, [(index, index ^ bits) for index in range(count)])


def across_x(value):
    return swap(value, "dp", 1)


def across_y(value):
    return swap(value, "ctx", 2)


def across_core(value):
    return swap(value, "ctx", 1)


def turned(value, axis, flag):
    return jnp.where(flag == 1, jnp.flip(value, axis), value)


def one_sequence(
    tokens,
    segment_ids,
    norm1_gain,
    norm1_shift,
    w_query,
    w_key,
    w_value,
    query_bias,
    value_bias,
    w_out,
    out_bias,
    norm2_gain,
    norm2_shift,
    w_up,
    up_bias,
    w_down,
    down_bias,
    out_grad,
):
    dps, ctxs, groups = (lax.axis_size(name) for name in ALL)
    owners = dps * ctxs
    at_x = lax.axis_index("dp")
    at_ctx = lax.axis_index("ctx")
    at_z = lax.axis_index("tensor")
    at_y, at_core = at_ctx // 2, at_ctx % 2
    span, model = tokens.shape[1:]
    length = span * ctxs
    heads = query_bias.shape[0]
    width = heads * HEAD_DIM
    shard = w_query.shape[0]
    hidden = w_up.shape[1]
    shared, shared_up = query_bias.shape[1], up_bias.shape[1]

    away = jnp.array([0, 4, 2, 6, 1, 5, 3, 7], jnp.int32)
    order = jnp.concatenate(
        [away ^ (at_x * ctxs + at_ctx), jnp.arange(4, dtype=jnp.int32) ^ at_ctx, at_z[None]]
    ).astype(jnp.int32)

    def to_slots(value):
        mine = lax.dynamic_slice_in_dim(value, at_z * ctxs, ctxs, axis=0)
        return [
            lax.dynamic_index_in_dim(mine, at_ctx ^ bits, 0, keepdims=False)
            for bits in range(ctxs)
        ]

    def exchanged(slots):
        return jnp.stack([slots[0]] + [swap(slots[bits], "ctx", bits) for bits in (1, 2, 3)])

    def to_spans(pieces):
        return place_slots(order, lax.all_gather(pieces, "tensor", axis=0, tiled=True))

    small = jnp.concatenate(
        [
            norm1_gain,
            norm1_shift,
            out_bias,
            norm2_gain,
            norm2_shift,
            down_bias,
            query_bias.reshape(-1),
            value_bias.reshape(-1),
            up_bias.reshape(-1),
        ]
    )
    used = small.shape[0]
    lanes = -(-used // (16 * 1024)) * 16 * 1024
    kept = -(-used // WIDE) * WIDE
    small = jnp.pad(small, (0, lanes - used)).reshape(-1, 1024)
    pack = jnp.concatenate([w_query, w_key, w_value, w_out.T], axis=1)
    cut = shard // 2
    pack = jnp.concatenate([pack, small], axis=0)
    lines = -(-span // 1024) * 8
    segs = jnp.pad(segment_ids, ((0, 0), (0, lines * WIDE - span))).reshape(-1, lines, WIDE)
    near, far, pieces, segs = gather_first(pack, tokens, segs, cut)
    small = jnp.stack([near[..., shard : shard + 16, :], far[..., shard : shard + 16, :]])
    small = small.reshape(2, 2, 2, groups, lanes)[..., :kept]
    pack_near, pack_far = (part.reshape((4,) + part.shape[2:]) for part in (near, far))
    segs = segs.reshape(2, 2, -1)[:, :, :span]
    segs = turned(turned(segs, 0, at_y), 1, at_core)
    weights = lax.all_gather(jnp.stack([w_up, w_down.T]), ALL, axis=0, tiled=False)

    vectors = small[:, :, :, 0, : 6 * shard].reshape(owners, 6, shard)
    vectors = vectors.transpose(1, 0, 2).reshape(6, 1, model).astype(jnp.float32)
    biases = turned(turned(turned(small, 0, at_core), 1, at_y), 2, at_x)
    biases = biases.transpose(2, 1, 0, 3, 4).reshape(owners, groups, kept)
    gain_one, shift_one, bias_out, gain_two, shift_two, bias_down = (
        vectors[index] for index in range(6)
    )

    def heads_bias(first, columns):
        part = biases[:, :, first : first + heads * columns]
        part = part.reshape(owners, groups, heads, columns).transpose(1, 2, 0, 3)
        return part.reshape(groups, 1, heads * columns * owners).astype(jnp.float32)

    first = 6 * shard
    bias_query = heads_bias(first, shared)
    bias_value = heads_bias(first + heads * shared, shared)
    bias_up = heads_bias(first + 2 * heads * shared, shared_up)
    bias_qkv = jnp.concatenate([bias_query, jnp.zeros_like(bias_query), bias_value], axis=2)

    seg_row = segs.reshape(1, 1, length)
    seg_col = segs.reshape(1, length, 1)
    head_place = (jnp.arange(groups)[:, None] ^ at_z) * heads + jnp.arange(heads)[None]
    slopes = jnp.exp2(-8.0 * (head_place.reshape(-1) + 1).astype(jnp.float32) / HEADS)

    x = order_pieces(order, pieces)
    h1, qkv = project(x, gain_one, shift_one, bias_qkv, pack_near, pack_far, 3 * width)
    grad_slots, qkv = lax.optimization_barrier((to_slots(out_grad), qkv))
    qkv = qkv.reshape(1, length, groups * 3 * width)
    mixed, log_total = attend(slopes, seg_row, seg_col, qkv, groups, heads)
    mixed = mixed.reshape(length, groups * width)
    x1, h2 = mix_out(mixed, x, bias_out, gain_two, shift_two, pack_near, pack_far, width)
    activated, gelu_slope = expand(order, h2, bias_up, weights)
    result = contract(order, activated, x1, bias_down, weights, groups)

    def away(left, right):
        return matmul_left(left[:, left.shape[1] // 2 :], right).astype(jnp.bfloat16)

    def home(left, right):
        return matmul_left(left[:, : left.shape[1] // 2], right)

    def add(here, there):
        total = here.astype(jnp.float32) + there.astype(jnp.float32)
        return total.astype(there.dtype)

    def over_xy(total, x_first, depth):
        total = total.reshape(2, 2, depth, -1)
        if x_first:
            total = add(total[:, 0], across_x(total[:, 1]))
            return add(total[0], across_y(total[1]))
        total = add(total[0], across_y(total[1]))
        return add(total[0], across_x(total[1]))

    def over_z(total):
        columns = total.shape[1] // groups
        result = total[:, :columns].astype(jnp.float32)
        for bits in (1, 2, 3):
            part = total[:, bits * columns : (bits + 1) * columns]
            result = result + swap(part, "tensor", bits).astype(jnp.float32)
        return result

    dy = order_pieces(order, exchanged(grad_slots))
    dy, result, activated = lax.optimization_barrier((dy, result, activated))
    result = exchanged(list(result))
    away_down = away(dy, activated)
    home_down = home(dy, activated).astype(jnp.bfloat16)
    dy, result, away_down, home_down = lax.optimization_barrier(
        (dy, result, away_down, home_down)
    )
    outputs = to_spans(result)
    da, grad_ubias, dx1, dattn, sums_two = ff_back(
        order, dy, gelu_slope, x1, gain_two, weights, groups
    )

    from_core = across_core(away_down)
    dattn, da, from_core = lax.optimization_barrier((dattn, da, from_core))
    down = add(home_down, from_core).reshape(2, 2, shard, -1)
    away_up = away(h2, da)
    from_core = across_core(away_up)
    do = mix_back(dattn, pack_near, pack_far, width)
    up = add(home(h2, da), from_core).reshape(2, 2, shard, -1)
    do, down, up = lax.optimization_barrier((do, down, up))
    down_part, up_part = across_y(down[1]), across_x(up[:, 1])
    dqkv = attend_back(
        slopes,
        seg_row,
        seg_col,
        qkv,
        do.reshape(1, length, groups * width),
        log_total,
        groups,
        heads,
    ).reshape(length, groups * 3 * width)
    dqkv, down_part, up_part = lax.optimization_barrier((dqkv, down_part, up_part))
    down, up = add(down[0], down_part), add(up[:, 0], up_part)
    down_part, up_part = across_x(down[1]), across_y(up[1])
    pieces_grad, grad_bias, sums_one = project_back(
        order, dqkv, x, dx1, gain_one, pack_near, pack_far, 3 * width
    )
    pieces_grad, down_part, up_part = lax.optimization_barrier((pieces_grad, down_part, up_part))
    sum_down = over_z(add(down[0], down_part)).T
    sum_up = over_z(add(up[0], up_part))
    pieces_grad = exchanged(list(pieces_grad))
    away_qkv = away(h1, dqkv)
    away_wout = away(dattn, mixed)
    pieces_grad, away_qkv, away_wout = lax.optimization_barrier(
        (pieces_grad, away_qkv, away_wout)
    )
    tokens_grad = to_spans(pieces_grad)
    qkv_sum = add(home(h1, dqkv), across_core(away_qkv))
    sum_qkv = over_z(over_xy(qkv_sum, True, shard))
    wout_sum = add(home(dattn, mixed), across_core(away_wout))
    sum_wout = over_z(over_xy(wout_sum, False, shard)).T

    grad_vectors = jnp.concatenate([sums_one, sums_two], axis=0)
    grad_vectors = grad_vectors.reshape(6, owners, shard).transpose(1, 0, 2)
    grad_vectors = grad_vectors.reshape(owners, 1, 6 * shard)
    grad_vectors = jnp.broadcast_to(grad_vectors, (owners, groups, 6 * shard))

    def owner_bias(value, columns):
        value = value.reshape(groups, heads, 2, 2, 2, columns).transpose(4, 3, 2, 0, 1, 5)
        value = turned(turned(turned(value, 0, at_core), 1, at_y), 2, at_x)
        return value.reshape(owners, groups, heads * columns)

    grad_bias = grad_bias.reshape(groups, 3, heads, HEAD_DIM)
    grad_small = jnp.concatenate(
        [
            grad_vectors,
            owner_bias(grad_bias[:, 0], shared),
            owner_bias(grad_bias[:, 2], shared),
            owner_bias(grad_ubias, shared_up),
            jnp.zeros((owners, groups, kept - used), jnp.float32),
        ],
        axis=2,
    )
    grad_small = grad_small.reshape(owners, groups * kept)
    small_sum = add(grad_small[:4], across_core(grad_small[4:]))
    sum_small = over_z(over_xy(small_sum, True, 1)).reshape(-1)
    sums = sum_small[: 6 * shard].reshape(6, shard)
    sum_biases = sum_small[6 * shard :]
    count = heads * shared
    return (
        outputs,
        tokens_grad,
        sums[0],
        sums[1],
        sum_qkv[:, :width],
        sum_qkv[:, width : 2 * width],
        sum_qkv[:, 2 * width :],
        sum_biases[:count].reshape(heads, shared),
        sum_biases[count : 2 * count].reshape(heads, shared),
        sum_wout,
        sums[2],
        sums[3],
        sums[4],
        sum_up,
        sum_biases[2 * count : 2 * count + heads * shared_up].reshape(heads, shared_up),
        sum_down,
        sums[5],
    )


def choose_plan(tokens, *others):
    sizes = tuple(lax.axis_size(name) for name in ALL)
    if sizes == (2, 4, 4) and tokens.shape[0] == 16 and tokens.shape[1] % TILE == 0:
        return one_sequence(tokens, *others)
    return shards(tokens, *others)


def solution(mesh):
    return jax.shard_map(
        choose_plan,
        mesh=mesh,
        in_specs=(
            P("dp", "ctx", None),
            P("dp", "ctx"),
            P(("dp", "ctx")),
            P(("dp", "ctx")),
            P(("dp", "ctx"), "tensor"),
            P(("dp", "ctx"), "tensor"),
            P(("dp", "ctx"), "tensor"),
            P("tensor", ("dp", "ctx")),
            P("tensor", ("dp", "ctx")),
            P("tensor", ("dp", "ctx")),
            P(("dp", "ctx")),
            P(("dp", "ctx")),
            P(("dp", "ctx")),
            P(("dp", "ctx"), "tensor"),
            P("tensor", ("dp", "ctx")),
            P("tensor", ("dp", "ctx")),
            P(("dp", "ctx")),
            P("dp", "ctx", None),
        ),
        out_specs=(
            P("dp", "ctx", None),
            P("dp", "ctx", None),
            P(("dp", "ctx")),
            P(("dp", "ctx")),
            P(("dp", "ctx"), "tensor"),
            P(("dp", "ctx"), "tensor"),
            P(("dp", "ctx"), "tensor"),
            P("tensor", ("dp", "ctx")),
            P("tensor", ("dp", "ctx")),
            P("tensor", ("dp", "ctx")),
            P(("dp", "ctx")),
            P(("dp", "ctx")),
            P(("dp", "ctx")),
            P(("dp", "ctx"), "tensor"),
            P("tensor", ("dp", "ctx")),
            P("tensor", ("dp", "ctx")),
            P(("dp", "ctx")),
        ),
        check_vma=False,
    )
```

```python
import functools
import math

import jax
import jax.numpy as jnp
from jax import lax
from jax.experimental import pallas as pl
from jax.experimental.pallas import tpu as pltpu
from jax.sharding import PartitionSpec as P

HEADS = 16
MICRO = 2
HEAD_DIM = 64


EPSILON = 1e-05


def layer_norm(values, gain, shift):
    centre = values - jnp.mean(values, axis=-1, keepdims=True)
    spread = jnp.mean(centre * centre, axis=-1, keepdims=True)
    return centre * lax.rsqrt(spread + EPSILON) * gain + shift


def gelu_tanh(values):
    return (
        0.5
        * values
        * (1.0 + jnp.tanh(0.7978845608028654 * (values + 0.044715 * values * values * values)))
    )


def matmul(left, right):
    return jnp.dot(left, right, preferred_element_type=jnp.float32)


def matmul_left(left, right):
    return lax.dot_general(
        left, right, (((0,), (0,)), ((), ())), preferred_element_type=jnp.float32
    )


def matmul_right(left, right):
    return lax.dot_general(
        left, right, (((1,), (1,)), ((), ())), preferred_element_type=jnp.float32
    )


def full_total(partial_value):
    return lax.psum(partial_value, "tensor")


def scores_of(query_heads, key_heads, query_seg, key_seg, slopes, query_first):
    query_count = query_heads.shape[1]
    key_count = key_heads.shape[1]
    head_width = query_heads.shape[3]
    raw_scores = jnp.einsum(
        "bqhd,bkhd->bhqk", query_heads, key_heads, preferred_element_type=jnp.float32
    )
    query_place = query_first + jnp.arange(query_count)
    key_place = jnp.arange(key_count)
    offsets = (key_place[None, :] - query_place[:, None]).astype(jnp.float32)
    scores = (
        raw_scores * (1.0 / math.sqrt(head_width))
        + slopes[None, :, None, None] * offsets[None, None]
    )
    causal = (key_place[None, :] <= query_place[:, None])[None, None]
    same_doc = query_seg[:, None, :, None] == key_seg[:, None, None, :]
    return jnp.where(causal & same_doc, scores, -1e30)


def shards(
    tokens,
    segment_ids,
    norm1_gain,
    norm1_shift,
    w_query,
    w_key,
    w_value,
    query_bias,
    value_bias,
    w_out,
    out_bias,
    norm2_gain,
    norm2_shift,
    w_up,
    up_bias,
    w_down,
    down_bias,
    out_grad,
):
    seqs_local, span_len, model_width = tokens.shape
    micro_seqs = seqs_local // MICRO
    row_count = micro_seqs * span_len
    heads_local = query_bias.shape[0]
    cols_local = heads_local * HEAD_DIM
    ff_local = w_up.shape[1]
    length_all = span_len * lax.axis_size("ctx")
    span_first = lax.axis_index("ctx") * span_len
    head_global = lax.axis_index("tensor") * heads_local + jnp.arange(heads_local)
    slopes = jnp.exp2(-8.0 * (head_global + 1).astype(jnp.float32) / HEADS)
    scale = 1.0 / math.sqrt(HEAD_DIM)
    grad_query = jnp.zeros((model_width, cols_local), jnp.float32)
    grad_key = jnp.zeros((model_width, cols_local), jnp.float32)
    grad_value = jnp.zeros((model_width, cols_local), jnp.float32)
    grad_qbias = jnp.zeros((heads_local, HEAD_DIM), jnp.float32)
    grad_vbias = jnp.zeros((heads_local, HEAD_DIM), jnp.float32)
    grad_wout = jnp.zeros((cols_local, model_width), jnp.float32)
    grad_small = jnp.zeros((6, model_width), jnp.float32)
    grad_up = jnp.zeros((model_width, ff_local), jnp.float32)
    grad_ubias = jnp.zeros((heads_local, ff_local // heads_local), jnp.float32)
    grad_down = jnp.zeros((ff_local, model_width), jnp.float32)
    outputs_list = []
    inputs_grad_list = []
    for micro_index in range(MICRO):
        first = micro_index * micro_seqs
        inputs = (
            tokens[first : first + micro_seqs].reshape(row_count, model_width).astype(jnp.float32)
        )
        query_seg = segment_ids[first : first + micro_seqs]
        cotangent = out_grad[first : first + micro_seqs].reshape(row_count, model_width)
        weights = (
            lax.all_gather(norm1_gain, ("dp", "ctx"), axis=0, tiled=True),
            lax.all_gather(norm1_shift, ("dp", "ctx"), axis=0, tiled=True),
            lax.all_gather(w_query, ("dp", "ctx"), axis=0, tiled=True),
            lax.all_gather(w_key, ("dp", "ctx"), axis=0, tiled=True),
            lax.all_gather(w_value, ("dp", "ctx"), axis=0, tiled=True),
            lax.all_gather(query_bias, ("dp", "ctx"), axis=1, tiled=True),
            lax.all_gather(value_bias, ("dp", "ctx"), axis=1, tiled=True),
            lax.all_gather(w_out, ("dp", "ctx"), axis=1, tiled=True),
            lax.all_gather(out_bias, ("dp", "ctx"), axis=0, tiled=True),
            lax.all_gather(norm2_gain, ("dp", "ctx"), axis=0, tiled=True),
            lax.all_gather(norm2_shift, ("dp", "ctx"), axis=0, tiled=True),
            lax.all_gather(w_up, ("dp", "ctx"), axis=0, tiled=True),
            lax.all_gather(up_bias, ("dp", "ctx"), axis=1, tiled=True),
            lax.all_gather(w_down, ("dp", "ctx"), axis=1, tiled=True),
            lax.all_gather(down_bias, ("dp", "ctx"), axis=0, tiled=True),
        )
        (
            gain_one,
            shift_one,
            full_query,
            full_key,
            full_value,
            bias_query,
            bias_value,
            full_out,
            bias_out,
            gain_two,
            shift_two,
            full_up,
            bias_up,
            full_down,
            bias_down,
        ) = weights
        gain_one = gain_one.astype(jnp.float32)
        shift_one = shift_one.astype(jnp.float32)
        gain_two = gain_two.astype(jnp.float32)
        shift_two = shift_two.astype(jnp.float32)
        bias_out = bias_out.astype(jnp.float32)
        bias_down = bias_down.astype(jnp.float32)
        normed_one = layer_norm(inputs, gain_one, shift_one).astype(jnp.bfloat16)
        queries = (
            matmul(normed_one, full_query) + bias_query.reshape(-1).astype(jnp.float32)
        ).astype(jnp.bfloat16)
        key_rows = matmul(normed_one, full_key).astype(jnp.bfloat16)
        value_rows = (
            matmul(normed_one, full_value) + bias_value.reshape(-1).astype(jnp.float32)
        ).astype(jnp.bfloat16)
        local_pairs = jnp.concatenate([key_rows, value_rows], axis=1).reshape(
            micro_seqs, span_len, 2 * cols_local
        )
        pairs_all, key_seg = (
            lax.all_gather(local_pairs, "ctx", axis=1, tiled=True),
            lax.all_gather(query_seg.astype(jnp.bfloat16), "ctx", axis=1, tiled=True),
        )
        key_seg = key_seg.astype(jnp.float32)
        query_segf = query_seg.astype(jnp.float32)
        key_heads = pairs_all[:, :, :cols_local].reshape(
            micro_seqs, length_all, heads_local, HEAD_DIM
        )
        value_heads = pairs_all[:, :, cols_local:].reshape(
            micro_seqs, length_all, heads_local, HEAD_DIM
        )
        query_heads = queries.reshape(micro_seqs, span_len, heads_local, HEAD_DIM)
        scores = scores_of(query_heads, key_heads, query_segf, key_seg, slopes, span_first)
        highest = jnp.max(scores, axis=-1, keepdims=True)
        exponent = jnp.exp(scores - highest)
        totals = jnp.sum(exponent, axis=-1, keepdims=True)
        softmaxed = exponent / totals
        log_total = highest + jnp.log(totals)
        mixed_heads = jnp.einsum(
            "bhqk,bkhd->bqhd",
            softmaxed.astype(jnp.bfloat16),
            value_heads,
            preferred_element_type=jnp.float32,
        )
        mixed_low = mixed_heads.reshape(row_count, cols_local).astype(jnp.bfloat16)
        attn_part = matmul(mixed_low, full_out)
        residual = inputs + full_total(attn_part) + bias_out
        normed_two = layer_norm(residual, gain_two, shift_two).astype(jnp.bfloat16)
        pre_act = matmul(normed_two, full_up) + bias_up.reshape(-1).astype(jnp.float32)
        activated = gelu_tanh(pre_act).astype(jnp.bfloat16)
        mlp_part = matmul(activated, full_down)
        result_rows = (residual + full_total(mlp_part) + bias_down).astype(jnp.bfloat16)
        outputs_list.append(result_rows.reshape(micro_seqs, span_len, model_width))
        weights_back = (
            lax.all_gather(norm1_gain, ("dp", "ctx"), axis=0, tiled=True),
            lax.all_gather(norm1_shift, ("dp", "ctx"), axis=0, tiled=True),
            lax.all_gather(w_query, ("dp", "ctx"), axis=0, tiled=True),
            lax.all_gather(w_key, ("dp", "ctx"), axis=0, tiled=True),
            lax.all_gather(w_value, ("dp", "ctx"), axis=0, tiled=True),
            lax.all_gather(query_bias, ("dp", "ctx"), axis=1, tiled=True),
            lax.all_gather(value_bias, ("dp", "ctx"), axis=1, tiled=True),
            lax.all_gather(w_out, ("dp", "ctx"), axis=1, tiled=True),
            lax.all_gather(out_bias, ("dp", "ctx"), axis=0, tiled=True),
            lax.all_gather(norm2_gain, ("dp", "ctx"), axis=0, tiled=True),
            lax.all_gather(norm2_shift, ("dp", "ctx"), axis=0, tiled=True),
            lax.all_gather(w_up, ("dp", "ctx"), axis=0, tiled=True),
            lax.all_gather(up_bias, ("dp", "ctx"), axis=1, tiled=True),
            lax.all_gather(w_down, ("dp", "ctx"), axis=1, tiled=True),
            lax.all_gather(down_bias, ("dp", "ctx"), axis=0, tiled=True),
        )
        back_query = weights_back[2]
        back_key = weights_back[3]
        back_value = weights_back[4]
        back_out = weights_back[7]
        back_up = weights_back[11]
        back_down = weights_back[13]
        gain_one = weights_back[0].astype(jnp.float32)
        shift_one = weights_back[1].astype(jnp.float32)
        gain_two = weights_back[9].astype(jnp.float32)
        shift_two = weights_back[10].astype(jnp.float32)
        act_grad = matmul_right(cotangent, back_down)
        unused, gelu_pull = jax.vjp(gelu_tanh, pre_act)
        pre_grad = gelu_pull(act_grad)[0].astype(jnp.bfloat16)
        grad_down = grad_down + matmul_left(activated, cotangent)
        grad_ubias = grad_ubias + jnp.sum(pre_grad.astype(jnp.float32), axis=0).reshape(
            heads_local, -1
        )
        grad_up = grad_up + matmul_left(normed_two, pre_grad)
        normed_two_back = matmul_right(pre_grad, back_up)
        unused, norm_pull = jax.vjp(layer_norm, residual, gain_two, shift_two)
        resid_grad, gain_two_grad, shift_two_grad = norm_pull(full_total(normed_two_back))
        cot_rows = cotangent.astype(jnp.float32)
        resid_grad = resid_grad + cot_rows
        attn_grad = resid_grad.astype(jnp.bfloat16)
        grad_wout = grad_wout + matmul_left(mixed_low, attn_grad)
        mixed_grad = matmul_right(attn_grad, back_out).astype(jnp.bfloat16)
        mixed_grad_heads = mixed_grad.reshape(micro_seqs, span_len, heads_local, HEAD_DIM)
        scores = scores_of(query_heads, key_heads, query_segf, key_seg, slopes, span_first)
        softmaxed = jnp.exp(scores - log_total)
        prob_grad = jnp.einsum(
            "bqhd,bkhd->bhqk", mixed_grad_heads, value_heads, preferred_element_type=jnp.float32
        )
        delta = jnp.sum(softmaxed * prob_grad, axis=-1, keepdims=True)
        score_grad = (softmaxed * (prob_grad - delta)).astype(jnp.bfloat16)
        query_grad = (
            jnp.einsum("bhqk,bkhd->bqhd", score_grad, key_heads, preferred_element_type=jnp.float32)
            * scale
        )
        query_low = query_grad.reshape(row_count, cols_local).astype(jnp.bfloat16)
        key_grad = (
            jnp.einsum(
                "bhqk,bqhd->bkhd", score_grad, query_heads, preferred_element_type=jnp.float32
            )
            * scale
        )
        value_grad = jnp.einsum(
            "bhqk,bqhd->bkhd",
            softmaxed.astype(jnp.bfloat16),
            mixed_grad_heads,
            preferred_element_type=jnp.float32,
        )
        pair_grad = jnp.concatenate(
            [
                key_grad.reshape(micro_seqs, length_all, cols_local),
                value_grad.reshape(micro_seqs, length_all, cols_local),
            ],
            axis=2,
        )
        pair_own = lax.psum_scatter(
            pair_grad.astype(jnp.bfloat16), "ctx", scatter_dimension=1, tiled=True
        ).astype(jnp.float32)
        key_low = pair_own[:, :, :cols_local].reshape(row_count, cols_local).astype(jnp.bfloat16)
        value_low = pair_own[:, :, cols_local:].reshape(row_count, cols_local).astype(jnp.bfloat16)
        grad_query = grad_query + matmul_left(normed_one, query_low)
        grad_key = grad_key + matmul_left(normed_one, key_low)
        grad_value = grad_value + matmul_left(normed_one, value_low)
        grad_qbias = grad_qbias + jnp.sum(query_low.astype(jnp.float32), axis=0).reshape(
            heads_local, HEAD_DIM
        )
        grad_vbias = grad_vbias + jnp.sum(value_low.astype(jnp.float32), axis=0).reshape(
            heads_local, HEAD_DIM
        )
        normed_one_back = (
            matmul_right(query_low, back_query)
            + matmul_right(key_low, back_key)
            + matmul_right(value_low, back_value)
        )
        unused, first_pull = jax.vjp(layer_norm, inputs, gain_one, shift_one)
        input_grad, gain_one_grad, shift_one_grad = first_pull(full_total(normed_one_back))
        input_grad = (input_grad + resid_grad).astype(jnp.bfloat16)
        inputs_grad_list.append(input_grad.reshape(micro_seqs, span_len, model_width))
        grad_small = grad_small + jnp.stack(
            [
                gain_one_grad,
                shift_one_grad,
                jnp.sum(resid_grad, axis=0),
                gain_two_grad,
                shift_two_grad,
                jnp.sum(cot_rows, axis=0),
            ],
            axis=0,
        )
    summed = (
        lax.psum_scatter(
            grad_query.astype(jnp.bfloat16), ("dp", "ctx"), scatter_dimension=0, tiled=True
        ).astype(jnp.float32),
        lax.psum_scatter(
            grad_key.astype(jnp.bfloat16), ("dp", "ctx"), scatter_dimension=0, tiled=True
        ).astype(jnp.float32),
        lax.psum_scatter(
            grad_value.astype(jnp.bfloat16), ("dp", "ctx"), scatter_dimension=0, tiled=True
        ).astype(jnp.float32),
        lax.psum_scatter(
            grad_qbias.astype(jnp.bfloat16), ("dp", "ctx"), scatter_dimension=1, tiled=True
        ).astype(jnp.float32),
        lax.psum_scatter(
            grad_vbias.astype(jnp.bfloat16), ("dp", "ctx"), scatter_dimension=1, tiled=True
        ).astype(jnp.float32),
        lax.psum_scatter(
            grad_wout.astype(jnp.bfloat16), ("dp", "ctx"), scatter_dimension=1, tiled=True
        ).astype(jnp.float32),
        lax.psum_scatter(
            grad_small.astype(jnp.bfloat16), ("dp", "ctx"), scatter_dimension=1, tiled=True
        ).astype(jnp.float32),
        lax.psum_scatter(
            grad_up.astype(jnp.bfloat16), ("dp", "ctx"), scatter_dimension=0, tiled=True
        ).astype(jnp.float32),
        lax.psum_scatter(
            grad_ubias.astype(jnp.bfloat16), ("dp", "ctx"), scatter_dimension=1, tiled=True
        ).astype(jnp.float32),
        lax.psum_scatter(
            grad_down.astype(jnp.bfloat16), ("dp", "ctx"), scatter_dimension=1, tiled=True
        ).astype(jnp.float32),
    )
    (
        sum_query,
        sum_key,
        sum_value,
        sum_qbias,
        sum_vbias,
        sum_wout,
        sum_small,
        sum_up,
        sum_ubias,
        sum_down,
    ) = summed
    return (
        jnp.concatenate(outputs_list, axis=0),
        jnp.concatenate(inputs_grad_list, axis=0),
        sum_small[0],
        sum_small[1],
        sum_query,
        sum_key,
        sum_value,
        sum_qbias,
        sum_vbias,
        sum_wout,
        sum_small[2],
        sum_small[3],
        sum_small[4],
        sum_up,
        sum_ubias,
        sum_down,
        sum_small[5],
    )


ALL = ("dp", "ctx", "tensor")
NORMAL = (((1,), (0,)), ((), ()))
ROWS = (((1,), (1,)), ((), ()))
COLS = (((0,), (0,)), ((), ()))
QUERY_BLOCK = 256


def dot(left, right, dims):
    return lax.dot_general(left, right, dims, preferred_element_type=jnp.float32)


def fill_distances(block, row_ref, col_ref, far_ref):
    @pl.when(pl.program_id(1) == 0)
    def _():
        for index in range(far_ref.shape[0]):
            first, last = index * block, (index + 1) * block
            key_place = lax.broadcasted_iota(jnp.int32, (last, 1), 0)
            query_place = first + lax.broadcasted_iota(jnp.int32, (1, block), 1)
            allowed = (key_place <= query_place) & (col_ref[0:last, :] == row_ref[:, first:last])
            distance = (key_place - query_place).astype(jnp.float32)
            far_ref[index, 0:last, :] = jnp.where(allowed, distance, -1e35)


def scaled(query):
    return (query.astype(jnp.float32) * (1.0 / math.sqrt(HEAD_DIM))).astype(jnp.bfloat16)


def attend_kernel(heads, block, slope_ref, row_ref, col_ref, qkv_ref, o_ref, lse_ref, far_ref):
    step = pl.program_id(1)
    length = qkv_ref.shape[0]
    width = heads * HEAD_DIM
    fill_distances(block, row_ref, col_ref, far_ref)
    for head in range(heads):
        lo = head * HEAD_DIM
        slope = slope_ref[step * heads + head]
        for first in range(0, length, block):
            last = first + block
            query = scaled(qkv_ref[first:last, lo : lo + HEAD_DIM])
            key = qkv_ref[0:last, width + lo : width + lo + HEAD_DIM]
            value = qkv_ref[0:last, 2 * width + lo : 2 * width + lo + HEAD_DIM]
            scores = dot(key, query, ROWS) + slope * far_ref[first // block, 0:last, :]
            highest = jnp.max(scores, axis=0, keepdims=True)
            exponent = jnp.exp(scores - highest)
            totals = jnp.sum(exponent, axis=0, keepdims=True)
            softmaxed = (exponent * (1.0 / totals)).astype(jnp.bfloat16)
            mixed = dot(softmaxed, value, COLS)
            o_ref[first:last, lo : lo + HEAD_DIM] = mixed.astype(jnp.bfloat16)
            lse_ref[head : head + 1, first:last] = highest + jnp.log(totals)


def attend_back_kernel(
    heads,
    block,
    slope_ref,
    row_ref,
    col_ref,
    qkv_ref,
    do_ref,
    lse_ref,
    grad_ref,
    dk_ref,
    dv_ref,
    far_ref,
):
    step = pl.program_id(1)
    length = qkv_ref.shape[0]
    width = heads * HEAD_DIM
    scale = 1.0 / math.sqrt(HEAD_DIM)
    fill_distances(block, row_ref, col_ref, far_ref)
    for head in range(heads):
        lo = head * HEAD_DIM
        slope = slope_ref[step * heads + head]
        for first in reversed(range(0, length, block)):
            last = first + block
            query = scaled(qkv_ref[first:last, lo : lo + HEAD_DIM])
            key = qkv_ref[0:last, width + lo : width + lo + HEAD_DIM]
            value = qkv_ref[0:last, 2 * width + lo : 2 * width + lo + HEAD_DIM]
            mixed_grad = do_ref[first:last, lo : lo + HEAD_DIM]
            scores = dot(key, query, ROWS) + slope * far_ref[first // block, 0:last, :]
            softmaxed = jnp.exp(scores - lse_ref[head : head + 1, first:last])
            prob_grad = dot(value, mixed_grad, ROWS)
            delta = jnp.sum(softmaxed * prob_grad, axis=0, keepdims=True)
            score_grad = (softmaxed * (prob_grad - delta)).astype(jnp.bfloat16)
            prob_low = softmaxed.astype(jnp.bfloat16)
            query_grad = dot(score_grad, key, COLS) * scale
            grad_ref[first:last, lo : lo + HEAD_DIM] = query_grad.astype(jnp.bfloat16)
            key_grad = dot(score_grad, query, NORMAL)
            value_grad = dot(prob_low, mixed_grad, NORMAL)
            if last == length:
                dk_ref[...] = key_grad
                dv_ref[...] = value_grad
            else:
                dk_ref[0:last, :] += key_grad
                dv_ref[0:last, :] += value_grad
        grad_ref[:, width + lo : width + lo + HEAD_DIM] = dk_ref[...].astype(jnp.bfloat16)
        grad_ref[:, 2 * width + lo : 2 * width + lo + HEAD_DIM] = dv_ref[...].astype(jnp.bfloat16)


def attention_specs(seqs, length, groups, heads):
    width = heads * HEAD_DIM
    return (
        pl.BlockSpec(memory_space=pltpu.SMEM),
        pl.BlockSpec((None, 1, length), lambda s, t: (s, 0, 0)),
        pl.BlockSpec((None, length, 1), lambda s, t: (s, 0, 0)),
        pl.BlockSpec((None, length, 3 * width), lambda s, t: (s, 0, t)),
        pl.BlockSpec((None, length, width), lambda s, t: (s, 0, t)),
        pl.BlockSpec((None, None, heads, length), lambda s, t: (s, t, 0, 0)),
    )


def attend(slopes, seg_row, seg_col, qkv, groups, heads):
    seqs, length, _ = qkv.shape
    specs = attention_specs(seqs, length, groups, heads)
    block = math.gcd(length, QUERY_BLOCK)
    return pl.pallas_call(
        functools.partial(attend_kernel, heads, block),
        grid=(seqs, groups),
        in_specs=list(specs[:4]),
        out_specs=[specs[4], specs[5]],
        out_shape=[
            jax.ShapeDtypeStruct((seqs, length, groups * heads * HEAD_DIM), jnp.bfloat16),
            jax.ShapeDtypeStruct((seqs, groups, heads, length), jnp.float32),
        ],
        scratch_shapes=[pltpu.VMEM((length // block, length, block), jnp.float32)],
        compiler_params=pltpu.CompilerParams(vmem_limit_bytes=40 * 2**20),
        cost_estimate=cost(4 * qkv.size * length, 4 * qkv.size),
        name="attend",
    )(slopes, seg_row, seg_col, qkv)


def attend_back(slopes, seg_row, seg_col, qkv, mixed_grad, log_total, groups, heads):
    seqs, length, _ = qkv.shape
    specs = attention_specs(seqs, length, groups, heads)
    block = math.gcd(length, QUERY_BLOCK)
    return pl.pallas_call(
        functools.partial(attend_back_kernel, heads, block),
        grid=(seqs, groups),
        in_specs=list(specs),
        out_specs=specs[3],
        out_shape=jax.ShapeDtypeStruct(qkv.shape, jnp.bfloat16),
        scratch_shapes=[
            pltpu.VMEM((length, HEAD_DIM), jnp.float32),
            pltpu.VMEM((length, HEAD_DIM), jnp.float32),
            pltpu.VMEM((length // block, length, block), jnp.float32),
        ],
        compiler_params=pltpu.CompilerParams(vmem_limit_bytes=40 * 2**20),
        cost_estimate=cost(4 * qkv.size * length, 4 * qkv.size),
        name="attend_back",
    )(slopes, seg_row, seg_col, qkv, mixed_grad, log_total)


def core_params(mib=56):
    return pltpu.CompilerParams(vmem_limit_bytes=mib * 2**20)


def cost(flops, moved):
    return pl.CostEstimate(
        flops=int(flops) // 64, bytes_accessed=int(moved) // 64, transcendentals=0
    )


TILE = 256
WEIGHT_ROWS = 128
WIDE = 128


def norm_parts(values):
    centre = values - jnp.mean(values, axis=-1, keepdims=True)
    spread = jnp.mean(centre * centre, axis=-1, keepdims=True)
    scale = lax.rsqrt(spread + EPSILON)
    return centre * scale, scale


def norm_back(grad, normed, scale, gain):
    scaled = grad * gain
    mean_one = jnp.mean(scaled, axis=-1, keepdims=True)
    mean_two = jnp.mean(scaled * normed, axis=-1, keepdims=True)
    return scale * (scaled - mean_one - normed * mean_two)


def column_sum(values):
    return jnp.sum(values, axis=0, keepdims=True)


def flat(ref):
    block = ref[...]
    return block.reshape(-1, block.shape[-1])


def joined(refs):
    blocks = [ref[...] for ref in refs]
    return jnp.concatenate(blocks[:4], axis=0), jnp.concatenate(blocks[4:], axis=0)


def ff_blocks(which, depth, hidden):
    def spec(block):
        def index(z, order):
            return (order[block] * 4 + lax.bitwise_xor(z, order[12]), which, 0, 0)

        return pl.BlockSpec((None, None, depth, hidden), index)

    return [spec(block) for block in range(8)]


def prefetched(grid, in_specs, out_specs, scratch=()):
    return pltpu.PrefetchScalarGridSpec(
        num_scalar_prefetch=1,
        grid=grid,
        in_specs=in_specs,
        out_specs=out_specs,
        scratch_shapes=list(scratch),
    )


def into_hidden(rows, near, far):
    half = rows.shape[1] // 2
    return dot(rows[:, :half], near, NORMAL) + dot(rows[:, half:], far, NORMAL)


def order_kernel(order_ref, pieces_ref, out_ref):
    columns = out_ref.shape[1] // WIDE
    for block in range(columns):
        place = pl.multiple_of(order_ref[block] * WIDE, WIDE)
        out_ref[:, block * WIDE : (block + 1) * WIDE] = pieces_ref[:, pl.ds(place, WIDE)]


def order_pieces(order, pieces):
    count, span, model = pieces.shape
    return pl.pallas_call(
        order_kernel,
        grid_spec=pltpu.PrefetchScalarGridSpec(
            num_scalar_prefetch=1,
            grid=(count,),
            in_specs=[pl.BlockSpec((None, span, model), lambda p, order: (order[8 + p], 0, 0))],
            out_specs=pl.BlockSpec((span, model), lambda p, order: (p, 0)),
        ),
        out_shape=jax.ShapeDtypeStruct((count * span, model), pieces.dtype),
        compiler_params=core_params(32),
        cost_estimate=cost(0, 4 * pieces.size),
        name="order_pieces",
    )(order, pieces)


def place_kernel(order_ref, one_ref, two_ref, out_ref):
    first = order_ref[8 + pl.program_id(1)] < 2

    @pl.when(first)
    def _():
        out_ref[...] = one_ref[...]

    @pl.when(jnp.logical_not(first))
    def _():
        out_ref[...] = two_ref[...]


def place_slots(order, one, two):
    count, span, model = one.shape

    def index_one(z, j, order):
        return (z * 2 + jnp.minimum(order[8 + j], 1), 0, 0)

    def index_two(z, j, order):
        return (z * 2 + jnp.maximum(order[8 + j] - 2, 0), 0, 0)

    block = (None, span, model)
    return pl.pallas_call(
        place_kernel,
        grid_spec=prefetched(
            (count // 2, 4),
            [pl.BlockSpec(block, index_one), pl.BlockSpec(block, index_two)],
            pl.BlockSpec(block, lambda z, j, order: (z * 4 + j, 0, 0)),
        ),
        out_shape=jax.ShapeDtypeStruct((2 * count, span, model), one.dtype),
        compiler_params=core_params(32),
        cost_estimate=cost(0, 8 * one.size),
        name="place_slots",
    )(order, one, two)


MESH = pl.DeviceIdType.MESH


def partner(place, bits):
    if bits == 3:
        return 3 - place
    return place + bits - 2 * bits * lax.rem(lax.div(place, bits), 2)


def gather_kernel(
    cut,
    pack_ref,
    tokens_ref,
    seg_ref,
    out_ref,
    far_ref,
    pieces_ref,
    segs_ref,
    local_sems,
    ctx_send,
    ctx_recv,
    z_send,
    z_recv,
    hop_send,
    hop_recv,
):
    at_x = lax.axis_index("dp")
    at_ctx = lax.axis_index("ctx")
    at_z = lax.axis_index("tensor")
    ctx_of = [{"ctx": partner(at_ctx, bits)} for bits in (1, 2, 3)]
    z_of = [{"tensor": partner(at_z, bits)} for bits in (1, 2, 3)]
    x_of, y_of, core_of = {"dp": 1 - at_x}, ctx_of[1], ctx_of[0]

    barrier = pltpu.get_barrier_semaphore()
    for device in ctx_of + z_of + [x_of]:
        pl.semaphore_signal(barrier, inc=1, device_id=device, device_id_type=MESH)
    pl.semaphore_wait(barrier, 7)

    def remote(source, target, send, recv, device):
        copy = pltpu.make_async_remote_copy(
            src_ref=source,
            dst_ref=target,
            send_sem=send,
            recv_sem=recv,
            device_id=device,
            device_id_type=MESH,
        )
        copy.start()
        return copy

    def hop(stage, z, source, target, device):
        return remote(source, target, hop_send.at[stage, z], hop_recv.at[stage, z], device)

    def slot(bits):
        place = at_ctx if bits == 0 else partner(at_ctx, bits)
        return at_z * 4 + place

    local = [
        pltpu.make_async_copy(pack_ref, out_ref.at[0, 0, 0], local_sems.at[0]),
        pltpu.make_async_copy(tokens_ref.at[slot(0)], pieces_ref.at[0], local_sems.at[1]),
        pltpu.make_async_copy(seg_ref.at[slot(0)], segs_ref.at[0], local_sems.at[2]),
    ]
    for copy in local:
        copy.start()
    across = [
        remote(pack_ref, out_ref.at[0, 0, bits], z_send.at[bits], z_recv.at[bits], z_of[bits - 1])
        for bits in (1, 2, 3)
    ]

    def first_hops(z, source):
        return (
            hop(0, z, source.at[:cut], out_ref.at[0, 1, z, :cut], x_of),
            hop(1, z, source.at[cut:], out_ref.at[1, 0, z, cut:], y_of),
        )

    first = [first_hops(0, pack_ref)]
    others = []
    for bits in (1, 2, 3):
        device = ctx_of[bits - 1]
        for kind, (source, target) in enumerate(((tokens_ref, pieces_ref), (seg_ref, segs_ref))):
            send, recv = ctx_send.at[kind, bits], ctx_recv.at[kind, bits]
            others.append(remote(source.at[slot(bits)], target.at[bits], send, recv, device))
    for z in (1, 2, 3):
        across[z - 1].wait_recv()
        first.append(first_hops(z, out_ref.at[0, 0, z]))
    local[0].wait()
    second = []
    for z in range(4):
        first[z][0].wait_recv()
        source = out_ref.at[0, :, z, :cut]
        to_y = hop(2, z, source, out_ref.at[1, :, z, :cut], y_of)
        first[z][1].wait_recv()
        source = out_ref.at[:, 0, z, cut:]
        second.append((to_y, hop(3, z, source, out_ref.at[:, 1, z, cut:], x_of)))
    third = []
    for z in range(4):
        for copy in second[z]:
            copy.wait_recv()
        third.append(hop(4, z, out_ref.at[:, :, z], far_ref.at[:, :, z], core_of))
    for copy in third + others:
        copy.wait_recv()
    for copy in across + others + third:
        copy.wait_send()
    for pair in first + second:
        for copy in pair:
            copy.wait_send()
    local[1].wait()
    local[2].wait()


def gather_first(pack, tokens, segs, cut):
    rows, columns = pack.shape
    span, model = tokens.shape[1:]
    anywhere = pl.BlockSpec(memory_space=pl.ANY)
    sems = pltpu.SemaphoreType.DMA
    return pl.pallas_call(
        functools.partial(gather_kernel, cut),
        in_specs=[anywhere] * 3,
        out_specs=[anywhere] * 4,
        out_shape=[
            jax.ShapeDtypeStruct((2, 2, 4, rows, columns), pack.dtype),
            jax.ShapeDtypeStruct((2, 2, 4, rows, columns), pack.dtype),
            jax.ShapeDtypeStruct((4, span, model), tokens.dtype),
            jax.ShapeDtypeStruct((4,) + segs.shape[1:], segs.dtype),
        ],
        scratch_shapes=[
            sems((3,)),
            sems((2, 4)),
            sems((2, 4)),
            sems((4,)),
            sems((4,)),
            sems((5, 4)),
            sems((5, 4)),
        ],
        compiler_params=pltpu.CompilerParams(collective_id=0, has_side_effects=True),
        cost_estimate=cost(0, 128 * 2**20),
        name="gather_first",
    )(pack, tokens, segs)


def whole(*shape):
    zeros = (0,) * len(shape)
    return pl.BlockSpec(shape, lambda *_: zeros)


def weight_block(rows, columns, index):
    return pl.BlockSpec((4, None, rows, columns), lambda z: (0, z, 0, index))


def project_kernel(x_ref, gain_ref, shift_ref, bias_ref, near_ref, far_ref, h_ref, out_ref):
    rows = x_ref.shape[0]

    @pl.when(pl.program_id(0) == 0)
    def _():
        for first in range(0, rows, TILE):
            normed, _ = norm_parts(x_ref[first : first + TILE].astype(jnp.float32))
            h_ref[first : first + TILE] = (normed * gain_ref[...] + shift_ref[...]).astype(
                jnp.bfloat16
            )

    near, far = flat(near_ref), flat(far_ref)
    for first in range(0, rows, TILE):
        sums = into_hidden(h_ref[first : first + TILE], near, far) + bias_ref[...]
        out_ref[first : first + TILE] = sums.astype(jnp.bfloat16)


def project(x, gain, shift, bias, near, far, width):
    rows, model = x.shape
    groups = near.shape[1]
    return pl.pallas_call(
        project_kernel,
        grid=(groups,),
        in_specs=[
            whole(rows, model),
            whole(1, model),
            whole(1, model),
            pl.BlockSpec((None, 1, width), lambda z: (z, 0, 0)),
            weight_block(WEIGHT_ROWS, width, 0),
            weight_block(WEIGHT_ROWS, width, 0),
        ],
        out_specs=[whole(rows, model), pl.BlockSpec((rows, width), lambda z: (0, z))],
        out_shape=[
            jax.ShapeDtypeStruct((rows, model), jnp.bfloat16),
            jax.ShapeDtypeStruct((rows, groups * width), jnp.bfloat16),
        ],
        compiler_params=core_params(),
        cost_estimate=cost(2 * rows * model * groups * width, 2 * model * groups * width),
        name="project",
    )(x, gain, shift, bias, near, far)


def mix_out_kernel(
    o_ref, x_ref, bias_ref, gain_ref, shift_ref, near_ref, far_ref, x1_ref, h_ref
):
    groups, width = near_ref.shape[1], near_ref.shape[3]
    halves = []
    for weights in (near_ref, far_ref):
        total = None
        for z in range(groups):
            block = weights[:, z].reshape(-1, width)
            part = dot(o_ref[:, z * width : (z + 1) * width], block, ROWS)
            total = part if total is None else total + part
        halves.append(total)
    residual = x_ref[...].astype(jnp.float32) + jnp.concatenate(halves, axis=1) + bias_ref[...]
    x1_ref[...] = residual
    normed, _ = norm_parts(residual)
    h_ref[...] = (normed * gain_ref[...] + shift_ref[...]).astype(jnp.bfloat16)


def mix_out(o, x, bias, gain, shift, near, far, width):
    rows, model = x.shape
    groups = near.shape[1]
    rowed = pl.BlockSpec((TILE, model), lambda r: (r, 0))
    weights = pl.BlockSpec((4, groups, WEIGHT_ROWS, width), lambda r: (0, 0, 0, 3))
    return pl.pallas_call(
        mix_out_kernel,
        grid=(rows // TILE,),
        in_specs=[rowed, rowed, whole(1, model), whole(1, model), whole(1, model)] + [weights] * 2,
        out_specs=[rowed, rowed],
        out_shape=[
            jax.ShapeDtypeStruct((rows, model), jnp.float32),
            jax.ShapeDtypeStruct((rows, model), jnp.bfloat16),
        ],
        compiler_params=core_params(),
        cost_estimate=cost(2 * rows * model * model, 12 * rows * model),
        name="mix_out",
    )(o, x, bias, gain, shift, near, far)


def expand_kernel(order_ref, h_ref, bias_ref, *refs):
    near, far = joined(refs[:8])
    g_ref, slope_ref = refs[8:]
    root = 0.7978845608028654
    for first in range(0, h_ref.shape[0], TILE):
        a = into_hidden(h_ref[first : first + TILE], near, far) + bias_ref[...]
        square = a * a
        bent = jnp.tanh(a * (root + (root * 0.044715) * square))
        half = 0.5 * a
        g_ref[first : first + TILE] = (half + half * bent).astype(jnp.bfloat16)
        inner = root + (3.0 * root * 0.044715) * square
        slope_ref[first : first + TILE] = (
            0.5 + 0.5 * bent + half * (1.0 - bent * bent) * inner
        ).astype(jnp.bfloat16)


def expand(order, h, bias, weights):
    rows, model = h.shape
    depth, hidden = weights.shape[2:]
    groups = bias.shape[0]
    out = pl.BlockSpec((rows, hidden), lambda z, order: (0, z))
    return pl.pallas_call(
        expand_kernel,
        grid_spec=prefetched(
            (groups,),
            [whole(rows, model), pl.BlockSpec((None, 1, hidden), lambda z, order: (z, 0, 0))]
            + ff_blocks(0, depth, hidden),
            [out, out],
        ),
        out_shape=[jax.ShapeDtypeStruct((rows, groups * hidden), jnp.bfloat16)] * 2,
        compiler_params=core_params(),
        cost_estimate=cost(2 * rows * model * groups * hidden, 8 * rows * groups * hidden),
        name="expand",
    )(order, h, bias, *[weights] * 8)


def contract_kernel(order_ref, g_ref, x1_ref, bias_ref, *refs):
    step = pl.program_id(0)
    near, far = joined(refs[:8])
    out_ref, total_ref = refs[8:]
    rows, model = total_ref.shape
    half = model // 2

    @pl.when(step == 0)
    def _():
        total_ref[...] = x1_ref[...] + bias_ref[...]

    for first in range(0, rows, TILE):
        part = g_ref[first : first + TILE]
        total_ref[first : first + TILE, :half] += dot(part, near, ROWS)
        total_ref[first : first + TILE, half:] += dot(part, far, ROWS)

    @pl.when(step == pl.num_programs(0) - 1)
    def _():
        store_absolute(order_ref, total_ref, out_ref)


def store_absolute(order_ref, value_ref, out_ref):
    span = out_ref.shape[1]
    for piece in range(out_ref.shape[0]):
        for block in range(out_ref.shape[2] // WIDE):
            place = pl.multiple_of(order_ref[block] * WIDE, WIDE)
            out_ref[order_ref[8 + piece], :, pl.ds(place, WIDE)] = value_ref[
                piece * span : (piece + 1) * span, block * WIDE : (block + 1) * WIDE
            ].astype(out_ref.dtype)


def contract(order, g, x1, bias, weights, groups):
    rows, model = x1.shape
    depth, hidden = weights.shape[2:]
    return pl.pallas_call(
        contract_kernel,
        grid_spec=prefetched(
            (groups,),
            [
                pl.BlockSpec((rows, hidden), lambda z, order: (0, z)),
                whole(rows, model),
                whole(1, model),
            ]
            + ff_blocks(1, depth, hidden),
            whole(4, rows // 4, model),
            [pltpu.VMEM((rows, model), jnp.float32)],
        ),
        out_shape=jax.ShapeDtypeStruct((4, rows // 4, model), jnp.bfloat16),
        compiler_params=core_params(),
        cost_estimate=cost(2 * rows * model * groups * hidden, 4 * rows * groups * hidden),
        name="contract",
    )(order, g, x1, bias, *[weights] * 8)


def ff_back_kernel(order_ref, dy_ref, slope_ref, x1_ref, gain_ref, *refs):
    step = pl.program_id(0)
    near, far = joined(refs[:8])
    up_one, up_two = joined(refs[8:16])
    da_ref, ubias_ref, dx1_ref, dattn_ref, sums_ref, total_ref = refs[16:]
    rows, model = total_ref.shape
    half = model // 2

    @pl.when(step == 0)
    def _():
        total_ref[...] = jnp.zeros_like(total_ref)

    sums = None
    for first in range(0, rows, TILE):
        span = slice(first, first + TILE)
        da = into_hidden(dy_ref[span], near, far) * slope_ref[span].astype(jnp.float32)
        da = da.astype(jnp.bfloat16)
        da_ref[span] = da
        part = column_sum(da.astype(jnp.float32))
        sums = part if sums is None else sums + part
        total_ref[span, :half] += dot(da, up_one, ROWS)
        total_ref[span, half:] += dot(da, up_two, ROWS)
    ubias_ref[...] = sums

    @pl.when(step == pl.num_programs(0) - 1)
    def _():
        gains = shifts = outs = downs = jnp.zeros((1, model), jnp.float32)
        for first in range(0, rows, TILE):
            span = slice(first, first + TILE)
            normed, scale = norm_parts(x1_ref[span])
            grad = total_ref[span]
            dy = dy_ref[span].astype(jnp.float32)
            gains = gains + column_sum(grad * normed)
            shifts = shifts + column_sum(grad)
            downs = downs + column_sum(dy)
            dx1 = dy + norm_back(grad, normed, scale, gain_ref[...])
            outs = outs + column_sum(dx1)
            dx1_ref[span] = dx1
            dattn_ref[span] = dx1.astype(jnp.bfloat16)
        sums_ref[...] = jnp.concatenate([outs, gains, shifts, downs], axis=0)


def ff_back(order, dy, slope, x1, gain, weights, groups):
    rows, model = x1.shape
    depth, hidden = weights.shape[2:]
    column = pl.BlockSpec((rows, hidden), lambda z, order: (0, z))
    return pl.pallas_call(
        ff_back_kernel,
        grid_spec=prefetched(
            (groups,),
            [whole(rows, model), column, whole(rows, model), whole(1, model)]
            + ff_blocks(1, depth, hidden)
            + ff_blocks(0, depth, hidden),
            [
                column,
                pl.BlockSpec((None, 1, hidden), lambda z, order: (z, 0, 0)),
                whole(rows, model),
                whole(rows, model),
                whole(4, model),
            ],
            [pltpu.VMEM((rows, model), jnp.float32)],
        ),
        out_shape=[
            jax.ShapeDtypeStruct((rows, groups * hidden), jnp.bfloat16),
            jax.ShapeDtypeStruct((groups, 1, hidden), jnp.float32),
            jax.ShapeDtypeStruct((rows, model), jnp.float32),
            jax.ShapeDtypeStruct((rows, model), jnp.bfloat16),
            jax.ShapeDtypeStruct((4, model), jnp.float32),
        ],
        compiler_params=core_params(60),
        cost_estimate=cost(4 * rows * model * groups * hidden, 8 * rows * groups * hidden),
        name="ff_back",
    )(order, dy, slope, x1, gain, *[weights] * 16)


def mix_back_kernel(dattn_ref, near_ref, far_ref, out_ref):
    near, far = flat(near_ref), flat(far_ref)
    out_ref[...] = into_hidden(dattn_ref[...], near, far).astype(jnp.bfloat16)


def mix_back(dattn, near, far, width):
    rows, model = dattn.shape
    groups = near.shape[1]
    return pl.pallas_call(
        mix_back_kernel,
        grid=(groups,),
        in_specs=[whole(rows, model)] + [weight_block(WEIGHT_ROWS, width, 3)] * 2,
        out_specs=pl.BlockSpec((rows, width), lambda z: (0, z)),
        out_shape=jax.ShapeDtypeStruct((rows, groups * width), jnp.bfloat16),
        compiler_params=core_params(),
        cost_estimate=cost(2 * rows * model * groups * width, 6 * rows * model),
        name="mix_back",
    )(dattn, near, far)


def project_back_kernel(
    order_ref,
    grad_ref,
    x_ref,
    dx1_ref,
    gain_ref,
    near_ref,
    far_ref,
    out_ref,
    bias_ref,
    sums_ref,
    total_ref,
):
    step = pl.program_id(0)
    rows, model = total_ref.shape
    half = model // 2
    near, far = flat(near_ref), flat(far_ref)

    @pl.when(step == 0)
    def _():
        total_ref[...] = jnp.zeros_like(total_ref)

    sums = None
    for first in range(0, rows, TILE):
        span = slice(first, first + TILE)
        grad = grad_ref[span]
        part = column_sum(grad.astype(jnp.float32))
        sums = part if sums is None else sums + part
        total_ref[span, :half] += dot(grad, near, ROWS)
        total_ref[span, half:] += dot(grad, far, ROWS)
    bias_ref[...] = sums

    @pl.when(step == pl.num_programs(0) - 1)
    def _():
        gains = shifts = jnp.zeros((1, model), jnp.float32)
        for first in range(0, rows, TILE):
            span = slice(first, first + TILE)
            normed, scale = norm_parts(x_ref[span].astype(jnp.float32))
            grad = total_ref[span]
            gains = gains + column_sum(grad * normed)
            shifts = shifts + column_sum(grad)
            total_ref[span] = dx1_ref[span] + norm_back(grad, normed, scale, gain_ref[...])
        sums_ref[...] = jnp.concatenate([gains, shifts], axis=0)
        store_absolute(order_ref, total_ref, out_ref)


def project_back(order, grad, x, dx1, gain, near, far, width):
    rows, model = x.shape
    groups = near.shape[1]
    return pl.pallas_call(
        project_back_kernel,
        grid=(groups,),
        in_specs=[
            pl.BlockSpec(memory_space=pltpu.SMEM),
            pl.BlockSpec((rows, width), lambda z: (0, z)),
            whole(rows, model),
            whole(rows, model),
            whole(1, model),
            weight_block(WEIGHT_ROWS, width, 0),
            weight_block(WEIGHT_ROWS, width, 0),
        ],
        out_specs=[
            whole(4, rows // 4, model),
            pl.BlockSpec((None, 1, width), lambda z: (z, 0, 0)),
            whole(2, model),
        ],
        out_shape=[
            jax.ShapeDtypeStruct((4, rows // 4, model), jnp.bfloat16),
            jax.ShapeDtypeStruct((groups, 1, width), jnp.float32),
            jax.ShapeDtypeStruct((2, model), jnp.float32),
        ],
        scratch_shapes=[pltpu.VMEM((rows, model), jnp.float32)],
        compiler_params=core_params(),
        cost_estimate=cost(2 * rows * model * groups * width, 8 * rows * model),
        name="project_back",
    )(order, grad, x, dx1, gain, near, far)


def swap(value, axis, bits):
    count = lax.axis_size(axis)
    return lax.ppermute(value, axis, [(index, index ^ bits) for index in range(count)])


def across_x(value):
    return swap(value, "dp", 1)


def across_y(value):
    return swap(value, "ctx", 2)


def across_core(value):
    return swap(value, "ctx", 1)


def turned(value, axis, flag):
    return jnp.where(flag == 1, jnp.flip(value, axis), value)


def one_sequence(
    tokens,
    segment_ids,
    norm1_gain,
    norm1_shift,
    w_query,
    w_key,
    w_value,
    query_bias,
    value_bias,
    w_out,
    out_bias,
    norm2_gain,
    norm2_shift,
    w_up,
    up_bias,
    w_down,
    down_bias,
    out_grad,
):
    dps, ctxs, groups = (lax.axis_size(name) for name in ALL)
    owners = dps * ctxs
    at_x = lax.axis_index("dp")
    at_ctx = lax.axis_index("ctx")
    at_z = lax.axis_index("tensor")
    at_y, at_core = at_ctx // 2, at_ctx % 2
    span, model = tokens.shape[1:]
    length = span * ctxs
    heads = query_bias.shape[0]
    width = heads * HEAD_DIM
    shard = w_query.shape[0]
    hidden = w_up.shape[1]
    shared, shared_up = query_bias.shape[1], up_bias.shape[1]

    away = jnp.array([0, 4, 2, 6, 1, 5, 3, 7], jnp.int32)
    order = jnp.concatenate(
        [away ^ (at_x * ctxs + at_ctx), jnp.arange(4, dtype=jnp.int32) ^ at_ctx, at_z[None]]
    ).astype(jnp.int32)

    def to_slots(value):
        mine = lax.dynamic_slice_in_dim(value, at_z * ctxs, ctxs, axis=0)
        return [
            lax.dynamic_index_in_dim(mine, at_ctx ^ bits, 0, keepdims=False)
            for bits in range(ctxs)
        ]

    def exchanged(slots):
        return jnp.stack([slots[0]] + [swap(slots[bits], "ctx", bits) for bits in (1, 2, 3)])

    def over_groups(pieces):
        return lax.all_gather(pieces, "tensor", axis=0, tiled=True)

    small = jnp.concatenate(
        [
            norm1_gain,
            norm1_shift,
            out_bias,
            norm2_gain,
            norm2_shift,
            down_bias,
            query_bias.reshape(-1),
            value_bias.reshape(-1),
            up_bias.reshape(-1),
        ]
    )
    used = small.shape[0]
    lanes = -(-used // (16 * 1024)) * 16 * 1024
    kept = -(-used // WIDE) * WIDE
    small = jnp.pad(small, (0, lanes - used)).reshape(-1, 1024)
    pack = jnp.concatenate([w_query, w_key, w_value, w_out.T], axis=1)
    cut = shard // 2
    pack = jnp.concatenate([pack, small], axis=0)
    lines = -(-span // 1024) * 8
    segs = jnp.pad(segment_ids, ((0, 0), (0, lines * WIDE - span))).reshape(-1, lines, WIDE)
    near, far, pieces, segs = gather_first(pack, tokens, segs, cut)
    small = jnp.stack([near[..., shard : shard + 16, :], far[..., shard : shard + 16, :]])
    small = small.reshape(2, 2, 2, groups, lanes)[..., :kept]
    pack_near, pack_far = (part.reshape((4,) + part.shape[2:]) for part in (near, far))
    segs = segs.reshape(2, 2, -1)[:, :, :span]
    segs = turned(turned(segs, 0, at_y), 1, at_core)
    weights = lax.all_gather(jnp.stack([w_up, w_down.T]), ALL, axis=0, tiled=False)

    vectors = small[:, :, :, 0, : 6 * shard].reshape(owners, 6, shard)
    vectors = vectors.transpose(1, 0, 2).reshape(6, 1, model).astype(jnp.float32)
    biases = turned(turned(turned(small, 0, at_core), 1, at_y), 2, at_x)
    biases = biases.transpose(2, 1, 0, 3, 4).reshape(owners, groups, kept)
    gain_one, shift_one, bias_out, gain_two, shift_two, bias_down = (
        vectors[index] for index in range(6)
    )

    def heads_bias(first, columns):
        part = biases[:, :, first : first + heads * columns]
        part = part.reshape(owners, groups, heads, columns).transpose(1, 2, 0, 3)
        return part.reshape(groups, 1, heads * columns * owners).astype(jnp.float32)

    first = 6 * shard
    bias_query = heads_bias(first, shared)
    bias_value = heads_bias(first + heads * shared, shared)
    bias_up = heads_bias(first + 2 * heads * shared, shared_up)
    bias_qkv = jnp.concatenate([bias_query, jnp.zeros_like(bias_query), bias_value], axis=2)

    seg_row = segs.reshape(1, 1, length)
    seg_col = segs.reshape(1, length, 1)
    head_place = (jnp.arange(groups)[:, None] ^ at_z) * heads + jnp.arange(heads)[None]
    slopes = jnp.exp2(-8.0 * (head_place.reshape(-1) + 1).astype(jnp.float32) / HEADS)

    x = order_pieces(order, pieces)
    h1, qkv = project(x, gain_one, shift_one, bias_qkv, pack_near, pack_far, 3 * width)
    grad_slots, qkv = lax.optimization_barrier((to_slots(out_grad), qkv))
    qkv = qkv.reshape(1, length, groups * 3 * width)
    mixed, log_total = attend(slopes, seg_row, seg_col, qkv, groups, heads)
    mixed = mixed.reshape(length, groups * width)
    x1, h2 = mix_out(mixed, x, bias_out, gain_two, shift_two, pack_near, pack_far, width)
    activated, gelu_slope = expand(order, h2, bias_up, weights)
    result = contract(order, activated, x1, bias_down, weights, groups)

    def away(left, right):
        return matmul_left(left[:, left.shape[1] // 2 :], right).astype(jnp.bfloat16)

    def home(left, right):
        return matmul_left(left[:, : left.shape[1] // 2], right)

    def add(here, there):
        total = here.astype(jnp.float32) + there.astype(jnp.float32)
        return total.astype(there.dtype)

    def over_xy(total, x_first, depth):
        total = total.reshape(2, 2, depth, -1)
        if x_first:
            total = add(total[:, 0], across_x(total[:, 1]))
            return add(total[0], across_y(total[1]))
        total = add(total[0], across_y(total[1]))
        return add(total[0], across_x(total[1]))

    def over_z(*totals):
        widths = [total.shape[1] // groups for total in totals]
        arrived = {}
        for step in range(1, groups):
            for sign in (1, -1):
                place = at_z if sign == 1 else groups - 1 - at_z
                target = jnp.minimum(groups - step + place, groups - 1)
                target = target if sign == 1 else groups - 1 - target
                pairs = [(index, index + 1) for index in range(step)]
                if sign == -1:
                    pairs = [(groups - 1 - here, groups - 1 - there) for here, there in pairs]
                for index, (total, columns) in enumerate(zip(totals, widths)):
                    part = lax.dynamic_slice_in_dim(
                        total, (target ^ at_z) * columns, columns, axis=1
                    )
                    if step > 1:
                        part = add(arrived[index, sign], part)
                    arrived[index, sign] = lax.ppermute(part, "tensor", pairs)
        return [
            total[:, :columns].astype(jnp.float32)
            + arrived[index, 1].astype(jnp.float32)
            + arrived[index, -1].astype(jnp.float32)
            for index, (total, columns) in enumerate(zip(totals, widths))
        ]

    dy = order_pieces(order, exchanged(grad_slots))
    dy, result, activated = lax.optimization_barrier((dy, result, activated))
    result = exchanged(list(result))
    away_down = away(dy, activated)
    home_down = home(dy, activated).astype(jnp.bfloat16)
    dy, result, away_down, home_down = lax.optimization_barrier(
        (dy, result, away_down, home_down)
    )
    result_one, result_two = over_groups(result[:2]), over_groups(result[2:])
    da, grad_ubias, dx1, dattn, sums_two = ff_back(
        order, dy, gelu_slope, x1, gain_two, weights, groups
    )

    from_core = across_core(away_down)
    dattn, da, from_core = lax.optimization_barrier((dattn, da, from_core))
    down = add(home_down, from_core).reshape(2, 2, shard, -1)
    do = mix_back(dattn, pack_near, pack_far, width)
    do, down = lax.optimization_barrier((do, down))
    down_part = across_y(down[1])
    dqkv = attend_back(
        slopes,
        seg_row,
        seg_col,
        qkv,
        do.reshape(1, length, groups * width),
        log_total,
        groups,
        heads,
    ).reshape(length, groups * 3 * width)
    dqkv, down_part, result_one = lax.optimization_barrier((dqkv, down_part, result_one))
    down = add(down[0], down_part)
    down_part = across_x(down[1])
    pieces_grad, grad_bias, sums_one = project_back(
        order, dqkv, x, dx1, gain_one, pack_near, pack_far, 3 * width
    )
    pieces_grad, h2, h1, dattn = lax.optimization_barrier((pieces_grad, h2, h1, dattn))
    pieces_grad = exchanged(list(pieces_grad))
    away_up = away(h2, da)
    away_qkv = away(h1, dqkv)
    away_wout = away(dattn, mixed)
    aways = away_up, away_qkv, away_wout
    pieces_grad, result_two, aways, down_part = lax.optimization_barrier(
        (pieces_grad, result_two, aways, down_part)
    )
    tokens_one, tokens_two = over_groups(pieces_grad[:2]), over_groups(pieces_grad[2:])
    outputs = place_slots(order, result_one, result_two)
    from_core = [across_core(part) for part in aways]
    up = add(home(h2, da), from_core[0]).reshape(2, 2, shard, -1)
    qkv_sum = add(home(h1, dqkv), from_core[1]).reshape(2, 2, shard, -1)
    wout_sum = add(home(dattn, mixed), from_core[2]).reshape(2, 2, shard, -1)
    down = add(down[0], down_part)
    up, qkv_sum, wout_sum, down = lax.optimization_barrier((up, qkv_sum, wout_sum, down))
    moved = across_x(up[:, 1]), across_y(qkv_sum[1]), across_y(wout_sum[1])
    (sum_down,) = over_z(down)
    sum_down = sum_down.T
    moved, sum_down = lax.optimization_barrier((moved, sum_down))
    up, qkv_sum, wout_sum = (
        add(up[:, 0], moved[0]),
        add(qkv_sum[0], moved[1]),
        add(wout_sum[0], moved[2]),
    )
    moved = across_y(up[1]), across_x(qkv_sum[1]), across_x(wout_sum[1])
    sum_up, sum_qkv, sum_wout = over_z(
        add(up[0], moved[0]), add(qkv_sum[0], moved[1]), add(wout_sum[0], moved[2])
    )
    sum_wout = sum_wout.T

    grad_vectors = jnp.concatenate([sums_one, sums_two], axis=0)
    grad_vectors = grad_vectors.reshape(6, owners, shard).transpose(1, 0, 2)
    grad_vectors = grad_vectors.reshape(owners, 1, 6 * shard)
    grad_vectors = jnp.broadcast_to(grad_vectors, (owners, groups, 6 * shard))

    def owner_bias(value, columns):
        value = value.reshape(groups, heads, 2, 2, 2, columns).transpose(4, 3, 2, 0, 1, 5)
        value = turned(turned(turned(value, 0, at_core), 1, at_y), 2, at_x)
        return value.reshape(owners, groups, heads * columns)

    grad_bias = grad_bias.reshape(groups, 3, heads, HEAD_DIM)
    grad_small = jnp.concatenate(
        [
            grad_vectors,
            owner_bias(grad_bias[:, 0], shared),
            owner_bias(grad_bias[:, 2], shared),
            owner_bias(grad_ubias, shared_up),
            jnp.zeros((owners, groups, kept - used), jnp.float32),
        ],
        axis=2,
    )
    grad_small = grad_small.reshape(owners, groups * kept)
    grad_small, sum_down = lax.optimization_barrier((grad_small, sum_down))
    small_sum = add(grad_small[:4], across_core(grad_small[4:]))
    sum_small = over_z(over_xy(small_sum, True, 1))[0].reshape(-1)
    tokens_one, tokens_two, sum_up, sum_qkv, sum_wout, sum_small = lax.optimization_barrier(
        (tokens_one, tokens_two, sum_up, sum_qkv, sum_wout, sum_small)
    )
    tokens_grad = place_slots(order, tokens_one, tokens_two)
    sums = sum_small[: 6 * shard].reshape(6, shard)
    sum_biases = sum_small[6 * shard :]
    count = heads * shared
    return (
        outputs,
        tokens_grad,
        sums[0],
        sums[1],
        sum_qkv[:, :width],
        sum_qkv[:, width : 2 * width],
        sum_qkv[:, 2 * width :],
        sum_biases[:count].reshape(heads, shared),
        sum_biases[count : 2 * count].reshape(heads, shared),
        sum_wout,
        sums[2],
        sums[3],
        sums[4],
        sum_up,
        sum_biases[2 * count : 2 * count + heads * shared_up].reshape(heads, shared_up),
        sum_down,
        sums[5],
    )


def choose_plan(tokens, *others):
    sizes = tuple(lax.axis_size(name) for name in ALL)
    if sizes == (2, 4, 4) and tokens.shape[0] == 16 and tokens.shape[1] % TILE == 0:
        return one_sequence(tokens, *others)
    return shards(tokens, *others)


def solution(mesh):
    return jax.shard_map(
        choose_plan,
        mesh=mesh,
        in_specs=(
            P("dp", "ctx", None),
            P("dp", "ctx"),
            P(("dp", "ctx")),
            P(("dp", "ctx")),
            P(("dp", "ctx"), "tensor"),
            P(("dp", "ctx"), "tensor"),
            P(("dp", "ctx"), "tensor"),
            P("tensor", ("dp", "ctx")),
            P("tensor", ("dp", "ctx")),
            P("tensor", ("dp", "ctx")),
            P(("dp", "ctx")),
            P(("dp", "ctx")),
            P(("dp", "ctx")),
            P(("dp", "ctx"), "tensor"),
            P("tensor", ("dp", "ctx")),
            P("tensor", ("dp", "ctx")),
            P(("dp", "ctx")),
            P("dp", "ctx", None),
        ),
        out_specs=(
            P("dp", "ctx", None),
            P("dp", "ctx", None),
            P(("dp", "ctx")),
            P(("dp", "ctx")),
            P(("dp", "ctx"), "tensor"),
            P(("dp", "ctx"), "tensor"),
            P(("dp", "ctx"), "tensor"),
            P("tensor", ("dp", "ctx")),
            P("tensor", ("dp", "ctx")),
            P("tensor", ("dp", "ctx")),
            P(("dp", "ctx")),
            P(("dp", "ctx")),
            P(("dp", "ctx")),
            P(("dp", "ctx"), "tensor"),
            P("tensor", ("dp", "ctx")),
            P("tensor", ("dp", "ctx")),
            P(("dp", "ctx")),
        ),
        check_vma=False,
    )
```

```python
import functools
import math

import jax
import jax.numpy as jnp
from jax import lax
from jax.experimental import pallas as pl
from jax.experimental.pallas import tpu as pltpu
from jax.sharding import PartitionSpec as P

HEADS = 16
MICRO = 2
HEAD_DIM = 64


EPSILON = 1e-05


def layer_norm(values, gain, shift):
    centre = values - jnp.mean(values, axis=-1, keepdims=True)
    spread = jnp.mean(centre * centre, axis=-1, keepdims=True)
    return centre * lax.rsqrt(spread + EPSILON) * gain + shift


def gelu_tanh(values):
    return (
        0.5
        * values
        * (1.0 + jnp.tanh(0.7978845608028654 * (values + 0.044715 * values * values * values)))
    )


def matmul(left, right):
    return jnp.dot(left, right, preferred_element_type=jnp.float32)


def matmul_left(left, right):
    return lax.dot_general(
        left, right, (((0,), (0,)), ((), ())), preferred_element_type=jnp.float32
    )


def matmul_right(left, right):
    return lax.dot_general(
        left, right, (((1,), (1,)), ((), ())), preferred_element_type=jnp.float32
    )


def full_total(partial_value):
    return lax.psum(partial_value, "tensor")


def scores_of(query_heads, key_heads, query_seg, key_seg, slopes, query_first):
    query_count = query_heads.shape[1]
    key_count = key_heads.shape[1]
    head_width = query_heads.shape[3]
    raw_scores = jnp.einsum(
        "bqhd,bkhd->bhqk", query_heads, key_heads, preferred_element_type=jnp.float32
    )
    query_place = query_first + jnp.arange(query_count)
    key_place = jnp.arange(key_count)
    offsets = (key_place[None, :] - query_place[:, None]).astype(jnp.float32)
    scores = (
        raw_scores * (1.0 / math.sqrt(head_width))
        + slopes[None, :, None, None] * offsets[None, None]
    )
    causal = (key_place[None, :] <= query_place[:, None])[None, None]
    same_doc = query_seg[:, None, :, None] == key_seg[:, None, None, :]
    return jnp.where(causal & same_doc, scores, -1e30)


def shards(
    tokens,
    segment_ids,
    norm1_gain,
    norm1_shift,
    w_query,
    w_key,
    w_value,
    query_bias,
    value_bias,
    w_out,
    out_bias,
    norm2_gain,
    norm2_shift,
    w_up,
    up_bias,
    w_down,
    down_bias,
    out_grad,
):
    seqs_local, span_len, model_width = tokens.shape
    micro_seqs = seqs_local // MICRO
    row_count = micro_seqs * span_len
    heads_local = query_bias.shape[0]
    cols_local = heads_local * HEAD_DIM
    ff_local = w_up.shape[1]
    length_all = span_len * lax.axis_size("ctx")
    span_first = lax.axis_index("ctx") * span_len
    head_global = lax.axis_index("tensor") * heads_local + jnp.arange(heads_local)
    slopes = jnp.exp2(-8.0 * (head_global + 1).astype(jnp.float32) / HEADS)
    scale = 1.0 / math.sqrt(HEAD_DIM)
    grad_query = jnp.zeros((model_width, cols_local), jnp.float32)
    grad_key = jnp.zeros((model_width, cols_local), jnp.float32)
    grad_value = jnp.zeros((model_width, cols_local), jnp.float32)
    grad_qbias = jnp.zeros((heads_local, HEAD_DIM), jnp.float32)
    grad_vbias = jnp.zeros((heads_local, HEAD_DIM), jnp.float32)
    grad_wout = jnp.zeros((cols_local, model_width), jnp.float32)
    grad_small = jnp.zeros((6, model_width), jnp.float32)
    grad_up = jnp.zeros((model_width, ff_local), jnp.float32)
    grad_ubias = jnp.zeros((heads_local, ff_local // heads_local), jnp.float32)
    grad_down = jnp.zeros((ff_local, model_width), jnp.float32)
    outputs_list = []
    inputs_grad_list = []
    for micro_index in range(MICRO):
        first = micro_index * micro_seqs
        inputs = (
            tokens[first : first + micro_seqs].reshape(row_count, model_width).astype(jnp.float32)
        )
        query_seg = segment_ids[first : first + micro_seqs]
        cotangent = out_grad[first : first + micro_seqs].reshape(row_count, model_width)
        weights = (
            lax.all_gather(norm1_gain, ("dp", "ctx"), axis=0, tiled=True),
            lax.all_gather(norm1_shift, ("dp", "ctx"), axis=0, tiled=True),
            lax.all_gather(w_query, ("dp", "ctx"), axis=0, tiled=True),
            lax.all_gather(w_key, ("dp", "ctx"), axis=0, tiled=True),
            lax.all_gather(w_value, ("dp", "ctx"), axis=0, tiled=True),
            lax.all_gather(query_bias, ("dp", "ctx"), axis=1, tiled=True),
            lax.all_gather(value_bias, ("dp", "ctx"), axis=1, tiled=True),
            lax.all_gather(w_out, ("dp", "ctx"), axis=1, tiled=True),
            lax.all_gather(out_bias, ("dp", "ctx"), axis=0, tiled=True),
            lax.all_gather(norm2_gain, ("dp", "ctx"), axis=0, tiled=True),
            lax.all_gather(norm2_shift, ("dp", "ctx"), axis=0, tiled=True),
            lax.all_gather(w_up, ("dp", "ctx"), axis=0, tiled=True),
            lax.all_gather(up_bias, ("dp", "ctx"), axis=1, tiled=True),
            lax.all_gather(w_down, ("dp", "ctx"), axis=1, tiled=True),
            lax.all_gather(down_bias, ("dp", "ctx"), axis=0, tiled=True),
        )
        (
            gain_one,
            shift_one,
            full_query,
            full_key,
            full_value,
            bias_query,
            bias_value,
            full_out,
            bias_out,
            gain_two,
            shift_two,
            full_up,
            bias_up,
            full_down,
            bias_down,
        ) = weights
        gain_one = gain_one.astype(jnp.float32)
        shift_one = shift_one.astype(jnp.float32)
        gain_two = gain_two.astype(jnp.float32)
        shift_two = shift_two.astype(jnp.float32)
        bias_out = bias_out.astype(jnp.float32)
        bias_down = bias_down.astype(jnp.float32)
        normed_one = layer_norm(inputs, gain_one, shift_one).astype(jnp.bfloat16)
        queries = (
            matmul(normed_one, full_query) + bias_query.reshape(-1).astype(jnp.float32)
        ).astype(jnp.bfloat16)
        key_rows = matmul(normed_one, full_key).astype(jnp.bfloat16)
        value_rows = (
            matmul(normed_one, full_value) + bias_value.reshape(-1).astype(jnp.float32)
        ).astype(jnp.bfloat16)
        local_pairs = jnp.concatenate([key_rows, value_rows], axis=1).reshape(
            micro_seqs, span_len, 2 * cols_local
        )
        pairs_all, key_seg = (
            lax.all_gather(local_pairs, "ctx", axis=1, tiled=True),
            lax.all_gather(query_seg.astype(jnp.bfloat16), "ctx", axis=1, tiled=True),
        )
        key_seg = key_seg.astype(jnp.float32)
        query_segf = query_seg.astype(jnp.float32)
        key_heads = pairs_all[:, :, :cols_local].reshape(
            micro_seqs, length_all, heads_local, HEAD_DIM
        )
        value_heads = pairs_all[:, :, cols_local:].reshape(
            micro_seqs, length_all, heads_local, HEAD_DIM
        )
        query_heads = queries.reshape(micro_seqs, span_len, heads_local, HEAD_DIM)
        scores = scores_of(query_heads, key_heads, query_segf, key_seg, slopes, span_first)
        highest = jnp.max(scores, axis=-1, keepdims=True)
        exponent = jnp.exp(scores - highest)
        totals = jnp.sum(exponent, axis=-1, keepdims=True)
        softmaxed = exponent / totals
        log_total = highest + jnp.log(totals)
        mixed_heads = jnp.einsum(
            "bhqk,bkhd->bqhd",
            softmaxed.astype(jnp.bfloat16),
            value_heads,
            preferred_element_type=jnp.float32,
        )
        mixed_low = mixed_heads.reshape(row_count, cols_local).astype(jnp.bfloat16)
        attn_part = matmul(mixed_low, full_out)
        residual = inputs + full_total(attn_part) + bias_out
        normed_two = layer_norm(residual, gain_two, shift_two).astype(jnp.bfloat16)
        pre_act = matmul(normed_two, full_up) + bias_up.reshape(-1).astype(jnp.float32)
        activated = gelu_tanh(pre_act).astype(jnp.bfloat16)
        mlp_part = matmul(activated, full_down)
        result_rows = (residual + full_total(mlp_part) + bias_down).astype(jnp.bfloat16)
        outputs_list.append(result_rows.reshape(micro_seqs, span_len, model_width))
        weights_back = (
            lax.all_gather(norm1_gain, ("dp", "ctx"), axis=0, tiled=True),
            lax.all_gather(norm1_shift, ("dp", "ctx"), axis=0, tiled=True),
            lax.all_gather(w_query, ("dp", "ctx"), axis=0, tiled=True),
            lax.all_gather(w_key, ("dp", "ctx"), axis=0, tiled=True),
            lax.all_gather(w_value, ("dp", "ctx"), axis=0, tiled=True),
            lax.all_gather(query_bias, ("dp", "ctx"), axis=1, tiled=True),
            lax.all_gather(value_bias, ("dp", "ctx"), axis=1, tiled=True),
            lax.all_gather(w_out, ("dp", "ctx"), axis=1, tiled=True),
            lax.all_gather(out_bias, ("dp", "ctx"), axis=0, tiled=True),
            lax.all_gather(norm2_gain, ("dp", "ctx"), axis=0, tiled=True),
            lax.all_gather(norm2_shift, ("dp", "ctx"), axis=0, tiled=True),
            lax.all_gather(w_up, ("dp", "ctx"), axis=0, tiled=True),
            lax.all_gather(up_bias, ("dp", "ctx"), axis=1, tiled=True),
            lax.all_gather(w_down, ("dp", "ctx"), axis=1, tiled=True),
            lax.all_gather(down_bias, ("dp", "ctx"), axis=0, tiled=True),
        )
        back_query = weights_back[2]
        back_key = weights_back[3]
        back_value = weights_back[4]
        back_out = weights_back[7]
        back_up = weights_back[11]
        back_down = weights_back[13]
        gain_one = weights_back[0].astype(jnp.float32)
        shift_one = weights_back[1].astype(jnp.float32)
        gain_two = weights_back[9].astype(jnp.float32)
        shift_two = weights_back[10].astype(jnp.float32)
        act_grad = matmul_right(cotangent, back_down)
        unused, gelu_pull = jax.vjp(gelu_tanh, pre_act)
        pre_grad = gelu_pull(act_grad)[0].astype(jnp.bfloat16)
        grad_down = grad_down + matmul_left(activated, cotangent)
        grad_ubias = grad_ubias + jnp.sum(pre_grad.astype(jnp.float32), axis=0).reshape(
            heads_local, -1
        )
        grad_up = grad_up + matmul_left(normed_two, pre_grad)
        normed_two_back = matmul_right(pre_grad, back_up)
        unused, norm_pull = jax.vjp(layer_norm, residual, gain_two, shift_two)
        resid_grad, gain_two_grad, shift_two_grad = norm_pull(full_total(normed_two_back))
        cot_rows = cotangent.astype(jnp.float32)
        resid_grad = resid_grad + cot_rows
        attn_grad = resid_grad.astype(jnp.bfloat16)
        grad_wout = grad_wout + matmul_left(mixed_low, attn_grad)
        mixed_grad = matmul_right(attn_grad, back_out).astype(jnp.bfloat16)
        mixed_grad_heads = mixed_grad.reshape(micro_seqs, span_len, heads_local, HEAD_DIM)
        scores = scores_of(query_heads, key_heads, query_segf, key_seg, slopes, span_first)
        softmaxed = jnp.exp(scores - log_total)
        prob_grad = jnp.einsum(
            "bqhd,bkhd->bhqk", mixed_grad_heads, value_heads, preferred_element_type=jnp.float32
        )
        delta = jnp.sum(softmaxed * prob_grad, axis=-1, keepdims=True)
        score_grad = (softmaxed * (prob_grad - delta)).astype(jnp.bfloat16)
        query_grad = (
            jnp.einsum("bhqk,bkhd->bqhd", score_grad, key_heads, preferred_element_type=jnp.float32)
            * scale
        )
        query_low = query_grad.reshape(row_count, cols_local).astype(jnp.bfloat16)
        key_grad = (
            jnp.einsum(
                "bhqk,bqhd->bkhd", score_grad, query_heads, preferred_element_type=jnp.float32
            )
            * scale
        )
        value_grad = jnp.einsum(
            "bhqk,bqhd->bkhd",
            softmaxed.astype(jnp.bfloat16),
            mixed_grad_heads,
            preferred_element_type=jnp.float32,
        )
        pair_grad = jnp.concatenate(
            [
                key_grad.reshape(micro_seqs, length_all, cols_local),
                value_grad.reshape(micro_seqs, length_all, cols_local),
            ],
            axis=2,
        )
        pair_own = lax.psum_scatter(
            pair_grad.astype(jnp.bfloat16), "ctx", scatter_dimension=1, tiled=True
        ).astype(jnp.float32)
        key_low = pair_own[:, :, :cols_local].reshape(row_count, cols_local).astype(jnp.bfloat16)
        value_low = pair_own[:, :, cols_local:].reshape(row_count, cols_local).astype(jnp.bfloat16)
        grad_query = grad_query + matmul_left(normed_one, query_low)
        grad_key = grad_key + matmul_left(normed_one, key_low)
        grad_value = grad_value + matmul_left(normed_one, value_low)
        grad_qbias = grad_qbias + jnp.sum(query_low.astype(jnp.float32), axis=0).reshape(
            heads_local, HEAD_DIM
        )
        grad_vbias = grad_vbias + jnp.sum(value_low.astype(jnp.float32), axis=0).reshape(
            heads_local, HEAD_DIM
        )
        normed_one_back = (
            matmul_right(query_low, back_query)
            + matmul_right(key_low, back_key)
            + matmul_right(value_low, back_value)
        )
        unused, first_pull = jax.vjp(layer_norm, inputs, gain_one, shift_one)
        input_grad, gain_one_grad, shift_one_grad = first_pull(full_total(normed_one_back))
        input_grad = (input_grad + resid_grad).astype(jnp.bfloat16)
        inputs_grad_list.append(input_grad.reshape(micro_seqs, span_len, model_width))
        grad_small = grad_small + jnp.stack(
            [
                gain_one_grad,
                shift_one_grad,
                jnp.sum(resid_grad, axis=0),
                gain_two_grad,
                shift_two_grad,
                jnp.sum(cot_rows, axis=0),
            ],
            axis=0,
        )
    summed = (
        lax.psum_scatter(
            grad_query.astype(jnp.bfloat16), ("dp", "ctx"), scatter_dimension=0, tiled=True
        ).astype(jnp.float32),
        lax.psum_scatter(
            grad_key.astype(jnp.bfloat16), ("dp", "ctx"), scatter_dimension=0, tiled=True
        ).astype(jnp.float32),
        lax.psum_scatter(
            grad_value.astype(jnp.bfloat16), ("dp", "ctx"), scatter_dimension=0, tiled=True
        ).astype(jnp.float32),
        lax.psum_scatter(
            grad_qbias.astype(jnp.bfloat16), ("dp", "ctx"), scatter_dimension=1, tiled=True
        ).astype(jnp.float32),
        lax.psum_scatter(
            grad_vbias.astype(jnp.bfloat16), ("dp", "ctx"), scatter_dimension=1, tiled=True
        ).astype(jnp.float32),
        lax.psum_scatter(
            grad_wout.astype(jnp.bfloat16), ("dp", "ctx"), scatter_dimension=1, tiled=True
        ).astype(jnp.float32),
        lax.psum_scatter(
            grad_small.astype(jnp.bfloat16), ("dp", "ctx"), scatter_dimension=1, tiled=True
        ).astype(jnp.float32),
        lax.psum_scatter(
            grad_up.astype(jnp.bfloat16), ("dp", "ctx"), scatter_dimension=0, tiled=True
        ).astype(jnp.float32),
        lax.psum_scatter(
            grad_ubias.astype(jnp.bfloat16), ("dp", "ctx"), scatter_dimension=1, tiled=True
        ).astype(jnp.float32),
        lax.psum_scatter(
            grad_down.astype(jnp.bfloat16), ("dp", "ctx"), scatter_dimension=1, tiled=True
        ).astype(jnp.float32),
    )
    (
        sum_query,
        sum_key,
        sum_value,
        sum_qbias,
        sum_vbias,
        sum_wout,
        sum_small,
        sum_up,
        sum_ubias,
        sum_down,
    ) = summed
    return (
        jnp.concatenate(outputs_list, axis=0),
        jnp.concatenate(inputs_grad_list, axis=0),
        sum_small[0],
        sum_small[1],
        sum_query,
        sum_key,
        sum_value,
        sum_qbias,
        sum_vbias,
        sum_wout,
        sum_small[2],
        sum_small[3],
        sum_small[4],
        sum_up,
        sum_ubias,
        sum_down,
        sum_small[5],
    )


ALL = ("dp", "ctx", "tensor")
NORMAL = (((1,), (0,)), ((), ()))
ROWS = (((1,), (1,)), ((), ()))
COLS = (((0,), (0,)), ((), ()))
QUERY_BLOCK = 256


def dot(left, right, dims):
    return lax.dot_general(left, right, dims, preferred_element_type=jnp.float32)


def fill_distances(block, row_ref, col_ref, far_ref):
    @pl.when(pl.program_id(1) == 0)
    def _():
        for index in range(far_ref.shape[0]):
            first, last = index * block, (index + 1) * block
            key_place = lax.broadcasted_iota(jnp.int32, (last, 1), 0)
            query_place = first + lax.broadcasted_iota(jnp.int32, (1, block), 1)
            allowed = (key_place <= query_place) & (col_ref[0:last, :] == row_ref[:, first:last])
            distance = (key_place - query_place).astype(jnp.float32)
            far_ref[index, 0:last, :] = jnp.where(allowed, distance, -1e35)


def scaled(query):
    return (query.astype(jnp.float32) * (1.0 / math.sqrt(HEAD_DIM))).astype(jnp.bfloat16)


def attend_kernel(heads, block, slope_ref, row_ref, col_ref, qkv_ref, o_ref, lse_ref, far_ref):
    step = pl.program_id(1)
    length = qkv_ref.shape[0]
    width = heads * HEAD_DIM
    fill_distances(block, row_ref, col_ref, far_ref)
    for head in range(heads):
        lo = head * HEAD_DIM
        slope = slope_ref[step * heads + head]
        for first in range(0, length, block):
            last = first + block
            query = scaled(qkv_ref[first:last, lo : lo + HEAD_DIM])
            key = qkv_ref[0:last, width + lo : width + lo + HEAD_DIM]
            value = qkv_ref[0:last, 2 * width + lo : 2 * width + lo + HEAD_DIM]
            scores = dot(key, query, ROWS) + slope * far_ref[first // block, 0:last, :]
            highest = jnp.max(scores, axis=0, keepdims=True)
            exponent = jnp.exp(scores - highest)
            totals = jnp.sum(exponent, axis=0, keepdims=True)
            softmaxed = (exponent * (1.0 / totals)).astype(jnp.bfloat16)
            mixed = dot(softmaxed, value, COLS)
            o_ref[first:last, lo : lo + HEAD_DIM] = mixed.astype(jnp.bfloat16)
            lse_ref[head : head + 1, first:last] = highest + jnp.log(totals)


def attend_back_kernel(
    heads,
    block,
    slope_ref,
    row_ref,
    col_ref,
    qkv_ref,
    do_ref,
    lse_ref,
    grad_ref,
    dk_ref,
    dv_ref,
    far_ref,
):
    step = pl.program_id(1)
    length = qkv_ref.shape[0]
    width = heads * HEAD_DIM
    scale = 1.0 / math.sqrt(HEAD_DIM)
    fill_distances(block, row_ref, col_ref, far_ref)
    for head in range(heads):
        lo = head * HEAD_DIM
        slope = slope_ref[step * heads + head]
        for first in reversed(range(0, length, block)):
            last = first + block
            query = scaled(qkv_ref[first:last, lo : lo + HEAD_DIM])
            key = qkv_ref[0:last, width + lo : width + lo + HEAD_DIM]
            value = qkv_ref[0:last, 2 * width + lo : 2 * width + lo + HEAD_DIM]
            mixed_grad = do_ref[first:last, lo : lo + HEAD_DIM]
            scores = dot(key, query, ROWS) + slope * far_ref[first // block, 0:last, :]
            softmaxed = jnp.exp(scores - lse_ref[head : head + 1, first:last])
            prob_grad = dot(value, mixed_grad, ROWS)
            delta = jnp.sum(softmaxed * prob_grad, axis=0, keepdims=True)
            score_grad = (softmaxed * (prob_grad - delta)).astype(jnp.bfloat16)
            prob_low = softmaxed.astype(jnp.bfloat16)
            query_grad = dot(score_grad, key, COLS) * scale
            grad_ref[first:last, lo : lo + HEAD_DIM] = query_grad.astype(jnp.bfloat16)
            key_grad = dot(score_grad, query, NORMAL)
            value_grad = dot(prob_low, mixed_grad, NORMAL)
            if last == length:
                dk_ref[...] = key_grad
                dv_ref[...] = value_grad
            else:
                dk_ref[0:last, :] += key_grad
                dv_ref[0:last, :] += value_grad
        grad_ref[:, width + lo : width + lo + HEAD_DIM] = dk_ref[...].astype(jnp.bfloat16)
        grad_ref[:, 2 * width + lo : 2 * width + lo + HEAD_DIM] = dv_ref[...].astype(jnp.bfloat16)


def attention_specs(seqs, length, groups, heads):
    width = heads * HEAD_DIM
    return (
        pl.BlockSpec(memory_space=pltpu.SMEM),
        pl.BlockSpec((None, 1, length), lambda s, t: (s, 0, 0)),
        pl.BlockSpec((None, length, 1), lambda s, t: (s, 0, 0)),
        pl.BlockSpec((None, length, 3 * width), lambda s, t: (s, 0, t)),
        pl.BlockSpec((None, length, width), lambda s, t: (s, 0, t)),
        pl.BlockSpec((None, None, heads, length), lambda s, t: (s, t, 0, 0)),
    )


def attend(slopes, seg_row, seg_col, qkv, groups, heads):
    seqs, length, _ = qkv.shape
    specs = attention_specs(seqs, length, groups, heads)
    block = math.gcd(length, QUERY_BLOCK)
    return pl.pallas_call(
        functools.partial(attend_kernel, heads, block),
        grid=(seqs, groups),
        in_specs=list(specs[:4]),
        out_specs=[specs[4], specs[5]],
        out_shape=[
            jax.ShapeDtypeStruct((seqs, length, groups * heads * HEAD_DIM), jnp.bfloat16),
            jax.ShapeDtypeStruct((seqs, groups, heads, length), jnp.float32),
        ],
        scratch_shapes=[pltpu.VMEM((length // block, length, block), jnp.float32)],
        compiler_params=pltpu.CompilerParams(vmem_limit_bytes=40 * 2**20),
        cost_estimate=cost(4 * qkv.size * length, 4 * qkv.size),
        name="attend",
    )(slopes, seg_row, seg_col, qkv)


def attend_back(slopes, seg_row, seg_col, qkv, mixed_grad, log_total, groups, heads):
    seqs, length, _ = qkv.shape
    specs = attention_specs(seqs, length, groups, heads)
    block = math.gcd(length, QUERY_BLOCK)
    return pl.pallas_call(
        functools.partial(attend_back_kernel, heads, block),
        grid=(seqs, groups),
        in_specs=list(specs),
        out_specs=specs[3],
        out_shape=jax.ShapeDtypeStruct(qkv.shape, jnp.bfloat16),
        scratch_shapes=[
            pltpu.VMEM((length, HEAD_DIM), jnp.float32),
            pltpu.VMEM((length, HEAD_DIM), jnp.float32),
            pltpu.VMEM((length // block, length, block), jnp.float32),
        ],
        compiler_params=pltpu.CompilerParams(vmem_limit_bytes=40 * 2**20),
        cost_estimate=cost(4 * qkv.size * length, 4 * qkv.size),
        name="attend_back",
    )(slopes, seg_row, seg_col, qkv, mixed_grad, log_total)


def core_params(mib=56):
    return pltpu.CompilerParams(vmem_limit_bytes=mib * 2**20)


def cost(flops, moved):
    return pl.CostEstimate(
        flops=int(flops) // 64, bytes_accessed=int(moved) // 64, transcendentals=0
    )


TILE = 256
WEIGHT_ROWS = 128
WIDE = 128


def norm_parts(values):
    centre = values - jnp.mean(values, axis=-1, keepdims=True)
    spread = jnp.mean(centre * centre, axis=-1, keepdims=True)
    scale = lax.rsqrt(spread + EPSILON)
    return centre * scale, scale


def norm_back(grad, normed, scale, gain):
    scaled = grad * gain
    mean_one = jnp.mean(scaled, axis=-1, keepdims=True)
    mean_two = jnp.mean(scaled * normed, axis=-1, keepdims=True)
    return scale * (scaled - mean_one - normed * mean_two)


def column_sum(values):
    return jnp.sum(values, axis=0, keepdims=True)


def flat(ref):
    block = ref[...]
    return block.reshape(-1, block.shape[-1])


def joined(refs):
    blocks = [ref[...] for ref in refs]
    return jnp.concatenate(blocks[:4], axis=0), jnp.concatenate(blocks[4:], axis=0)


def ff_blocks(which, depth, hidden):
    def spec(block):
        def index(z, order):
            return (order[block] * 4 + lax.bitwise_xor(z, order[12]), which, 0, 0)

        return pl.BlockSpec((None, None, depth, hidden), index)

    return [spec(block) for block in range(8)]


def prefetched(grid, in_specs, out_specs, scratch=()):
    return pltpu.PrefetchScalarGridSpec(
        num_scalar_prefetch=1,
        grid=grid,
        in_specs=in_specs,
        out_specs=out_specs,
        scratch_shapes=list(scratch),
    )


def into_hidden(rows, near, far):
    half = rows.shape[1] // 2
    return dot(rows[:, :half], near, NORMAL) + dot(rows[:, half:], far, NORMAL)


def order_kernel(order_ref, pieces_ref, out_ref):
    columns = out_ref.shape[1] // WIDE
    for block in range(columns):
        place = pl.multiple_of(order_ref[block] * WIDE, WIDE)
        out_ref[:, block * WIDE : (block + 1) * WIDE] = pieces_ref[:, pl.ds(place, WIDE)]


def order_pieces(order, pieces):
    count, span, model = pieces.shape
    return pl.pallas_call(
        order_kernel,
        grid_spec=pltpu.PrefetchScalarGridSpec(
            num_scalar_prefetch=1,
            grid=(count,),
            in_specs=[pl.BlockSpec((None, span, model), lambda p, order: (order[8 + p], 0, 0))],
            out_specs=pl.BlockSpec((span, model), lambda p, order: (p, 0)),
        ),
        out_shape=jax.ShapeDtypeStruct((count * span, model), pieces.dtype),
        compiler_params=core_params(32),
        cost_estimate=cost(0, 4 * pieces.size),
        name="order_pieces",
    )(order, pieces)


def place_kernel(order_ref, one_ref, two_ref, out_ref):
    first = order_ref[8 + pl.program_id(1)] < 2

    @pl.when(first)
    def _():
        out_ref[...] = one_ref[...]

    @pl.when(jnp.logical_not(first))
    def _():
        out_ref[...] = two_ref[...]


def place_slots(order, one, two):
    count, span, model = one.shape

    def index_one(z, j, order):
        return (z * 2 + jnp.minimum(order[8 + j], 1), 0, 0)

    def index_two(z, j, order):
        return (z * 2 + jnp.maximum(order[8 + j] - 2, 0), 0, 0)

    block = (None, span, model)
    return pl.pallas_call(
        place_kernel,
        grid_spec=prefetched(
            (count // 2, 4),
            [pl.BlockSpec(block, index_one), pl.BlockSpec(block, index_two)],
            pl.BlockSpec(block, lambda z, j, order: (z * 4 + j, 0, 0)),
        ),
        out_shape=jax.ShapeDtypeStruct((2 * count, span, model), one.dtype),
        compiler_params=core_params(32),
        cost_estimate=cost(0, 8 * one.size),
        name="place_slots",
    )(order, one, two)


MESH = pl.DeviceIdType.MESH


def partner(place, bits):
    if bits == 3:
        return 3 - place
    return place + bits - 2 * bits * lax.rem(lax.div(place, bits), 2)


def gather_kernel(
    cut,
    pack_ref,
    tokens_ref,
    seg_ref,
    out_ref,
    far_ref,
    pieces_ref,
    segs_ref,
    local_sems,
    ctx_send,
    ctx_recv,
    z_send,
    z_recv,
    hop_send,
    hop_recv,
):
    at_x = lax.axis_index("dp")
    at_ctx = lax.axis_index("ctx")
    at_z = lax.axis_index("tensor")
    ctx_of = [{"ctx": partner(at_ctx, bits)} for bits in (1, 2, 3)]
    z_of = [{"tensor": partner(at_z, bits)} for bits in (1, 2, 3)]
    x_of, y_of, core_of = {"dp": 1 - at_x}, ctx_of[1], ctx_of[0]

    barrier = pltpu.get_barrier_semaphore()
    for device in ctx_of + z_of + [x_of]:
        pl.semaphore_signal(barrier, inc=1, device_id=device, device_id_type=MESH)
    pl.semaphore_wait(barrier, 7)

    def remote(source, target, send, recv, device):
        copy = pltpu.make_async_remote_copy(
            src_ref=source,
            dst_ref=target,
            send_sem=send,
            recv_sem=recv,
            device_id=device,
            device_id_type=MESH,
        )
        copy.start()
        return copy

    def hop(stage, z, source, target, device):
        return remote(source, target, hop_send.at[stage, z], hop_recv.at[stage, z], device)

    def slot(bits):
        place = at_ctx if bits == 0 else partner(at_ctx, bits)
        return at_z * 4 + place

    local = [
        pltpu.make_async_copy(pack_ref, out_ref.at[0, 0, 0], local_sems.at[0]),
        pltpu.make_async_copy(tokens_ref.at[slot(0)], pieces_ref.at[0], local_sems.at[1]),
        pltpu.make_async_copy(seg_ref.at[slot(0)], segs_ref.at[0], local_sems.at[2]),
    ]
    for copy in local:
        copy.start()
    across = [
        remote(pack_ref, out_ref.at[0, 0, bits], z_send.at[bits], z_recv.at[bits], z_of[bits - 1])
        for bits in (1, 2, 3)
    ]

    def first_hops(z, source):
        return (
            hop(0, z, source.at[:cut], out_ref.at[0, 1, z, :cut], x_of),
            hop(1, z, source.at[cut:], out_ref.at[1, 0, z, cut:], y_of),
        )

    first = [first_hops(0, pack_ref)]
    others = []
    for bits in (1, 2, 3):
        device = ctx_of[bits - 1]
        for kind, (source, target) in enumerate(((tokens_ref, pieces_ref), (seg_ref, segs_ref))):
            send, recv = ctx_send.at[kind, bits], ctx_recv.at[kind, bits]
            others.append(remote(source.at[slot(bits)], target.at[bits], send, recv, device))
    for z in (1, 2, 3):
        across[z - 1].wait_recv()
        first.append(first_hops(z, out_ref.at[0, 0, z]))
    local[0].wait()
    second = []
    for z in range(4):
        first[z][0].wait_recv()
        source = out_ref.at[0, :, z, :cut]
        to_y = hop(2, z, source, out_ref.at[1, :, z, :cut], y_of)
        first[z][1].wait_recv()
        source = out_ref.at[:, 0, z, cut:]
        second.append((to_y, hop(3, z, source, out_ref.at[:, 1, z, cut:], x_of)))
    third = []
    for z in range(4):
        for copy in second[z]:
            copy.wait_recv()
        third.append(hop(4, z, out_ref.at[:, :, z], far_ref.at[:, :, z], core_of))
    for copy in third + others:
        copy.wait_recv()
    for copy in across + others + third:
        copy.wait_send()
    for pair in first + second:
        for copy in pair:
            copy.wait_send()
    local[1].wait()
    local[2].wait()


def gather_first(pack, tokens, segs, cut):
    rows, columns = pack.shape
    span, model = tokens.shape[1:]
    anywhere = pl.BlockSpec(memory_space=pl.ANY)
    sems = pltpu.SemaphoreType.DMA
    return pl.pallas_call(
        functools.partial(gather_kernel, cut),
        in_specs=[anywhere] * 3,
        out_specs=[anywhere] * 4,
        out_shape=[
            jax.ShapeDtypeStruct((2, 2, 4, rows, columns), pack.dtype),
            jax.ShapeDtypeStruct((2, 2, 4, rows, columns), pack.dtype),
            jax.ShapeDtypeStruct((4, span, model), tokens.dtype),
            jax.ShapeDtypeStruct((4,) + segs.shape[1:], segs.dtype),
        ],
        scratch_shapes=[
            sems((3,)),
            sems((2, 4)),
            sems((2, 4)),
            sems((4,)),
            sems((4,)),
            sems((5, 4)),
            sems((5, 4)),
        ],
        compiler_params=pltpu.CompilerParams(collective_id=0, has_side_effects=True),
        cost_estimate=cost(0, 128 * 2**20),
        name="gather_first",
    )(pack, tokens, segs)


def whole(*shape):
    zeros = (0,) * len(shape)
    return pl.BlockSpec(shape, lambda *_: zeros)


def weight_block(rows, columns, index):
    return pl.BlockSpec((4, None, rows, columns), lambda z: (0, z, 0, index))


def project_kernel(x_ref, gain_ref, shift_ref, bias_ref, near_ref, far_ref, h_ref, out_ref):
    rows = x_ref.shape[0]

    @pl.when(pl.program_id(0) == 0)
    def _():
        for first in range(0, rows, TILE):
            normed, _ = norm_parts(x_ref[first : first + TILE].astype(jnp.float32))
            h_ref[first : first + TILE] = (normed * gain_ref[...] + shift_ref[...]).astype(
                jnp.bfloat16
            )

    near, far = flat(near_ref), flat(far_ref)
    for first in range(0, rows, TILE):
        sums = into_hidden(h_ref[first : first + TILE], near, far) + bias_ref[...]
        out_ref[first : first + TILE] = sums.astype(jnp.bfloat16)


def project(x, gain, shift, bias, near, far, width):
    rows, model = x.shape
    groups = near.shape[1]
    return pl.pallas_call(
        project_kernel,
        grid=(groups,),
        in_specs=[
            whole(rows, model),
            whole(1, model),
            whole(1, model),
            pl.BlockSpec((None, 1, width), lambda z: (z, 0, 0)),
            weight_block(WEIGHT_ROWS, width, 0),
            weight_block(WEIGHT_ROWS, width, 0),
        ],
        out_specs=[whole(rows, model), pl.BlockSpec((rows, width), lambda z: (0, z))],
        out_shape=[
            jax.ShapeDtypeStruct((rows, model), jnp.bfloat16),
            jax.ShapeDtypeStruct((rows, groups * width), jnp.bfloat16),
        ],
        compiler_params=core_params(),
        cost_estimate=cost(2 * rows * model * groups * width, 2 * model * groups * width),
        name="project",
    )(x, gain, shift, bias, near, far)


def mix_out_kernel(
    o_ref, x_ref, bias_ref, gain_ref, shift_ref, near_ref, far_ref, x1_ref, h_ref
):
    groups, width = near_ref.shape[1], near_ref.shape[3]
    halves = []
    for weights in (near_ref, far_ref):
        total = None
        for z in range(groups):
            block = weights[:, z].reshape(-1, width)
            part = dot(o_ref[:, z * width : (z + 1) * width], block, ROWS)
            total = part if total is None else total + part
        halves.append(total)
    residual = x_ref[...].astype(jnp.float32) + jnp.concatenate(halves, axis=1) + bias_ref[...]
    x1_ref[...] = residual
    normed, _ = norm_parts(residual)
    h_ref[...] = (normed * gain_ref[...] + shift_ref[...]).astype(jnp.bfloat16)


def mix_out(o, x, bias, gain, shift, near, far, width):
    rows, model = x.shape
    groups = near.shape[1]
    rowed = pl.BlockSpec((TILE, model), lambda r: (r, 0))
    weights = pl.BlockSpec((4, groups, WEIGHT_ROWS, width), lambda r: (0, 0, 0, 3))
    return pl.pallas_call(
        mix_out_kernel,
        grid=(rows // TILE,),
        in_specs=[rowed, rowed, whole(1, model), whole(1, model), whole(1, model)] + [weights] * 2,
        out_specs=[rowed, rowed],
        out_shape=[
            jax.ShapeDtypeStruct((rows, model), jnp.float32),
            jax.ShapeDtypeStruct((rows, model), jnp.bfloat16),
        ],
        compiler_params=core_params(),
        cost_estimate=cost(2 * rows * model * model, 12 * rows * model),
        name="mix_out",
    )(o, x, bias, gain, shift, near, far)


def expand_kernel(order_ref, h_ref, bias_ref, *refs):
    near, far = joined(refs[:8])
    g_ref, slope_ref = refs[8:]
    root = 0.7978845608028654
    for first in range(0, h_ref.shape[0], TILE):
        a = into_hidden(h_ref[first : first + TILE], near, far) + bias_ref[...]
        square = a * a
        bent = jnp.tanh(a * (root + (root * 0.044715) * square))
        half = 0.5 * a
        g_ref[first : first + TILE] = (half + half * bent).astype(jnp.bfloat16)
        inner = root + (3.0 * root * 0.044715) * square
        slope_ref[first : first + TILE] = (
            0.5 + 0.5 * bent + half * (1.0 - bent * bent) * inner
        ).astype(jnp.bfloat16)


def expand(order, h, bias, weights):
    rows, model = h.shape
    depth, hidden = weights.shape[2:]
    groups = bias.shape[0]
    out = pl.BlockSpec((rows, hidden), lambda z, order: (0, z))
    return pl.pallas_call(
        expand_kernel,
        grid_spec=prefetched(
            (groups,),
            [whole(rows, model), pl.BlockSpec((None, 1, hidden), lambda z, order: (z, 0, 0))]
            + ff_blocks(0, depth, hidden),
            [out, out],
        ),
        out_shape=[jax.ShapeDtypeStruct((rows, groups * hidden), jnp.bfloat16)] * 2,
        compiler_params=core_params(),
        cost_estimate=cost(2 * rows * model * groups * hidden, 8 * rows * groups * hidden),
        name="expand",
    )(order, h, bias, *[weights] * 8)


def contract_kernel(order_ref, g_ref, x1_ref, bias_ref, *refs):
    step = pl.program_id(0)
    near, far = joined(refs[:8])
    out_ref, total_ref = refs[8:]
    rows, model = total_ref.shape
    half = model // 2

    @pl.when(step == 0)
    def _():
        total_ref[...] = x1_ref[...] + bias_ref[...]

    for first in range(0, rows, TILE):
        part = g_ref[first : first + TILE]
        total_ref[first : first + TILE, :half] += dot(part, near, ROWS)
        total_ref[first : first + TILE, half:] += dot(part, far, ROWS)

    @pl.when(step == pl.num_programs(0) - 1)
    def _():
        store_absolute(order_ref, total_ref, out_ref)


def store_absolute(order_ref, value_ref, out_ref):
    span = out_ref.shape[1]
    for piece in range(out_ref.shape[0]):
        for block in range(out_ref.shape[2] // WIDE):
            place = pl.multiple_of(order_ref[block] * WIDE, WIDE)
            out_ref[order_ref[8 + piece], :, pl.ds(place, WIDE)] = value_ref[
                piece * span : (piece + 1) * span, block * WIDE : (block + 1) * WIDE
            ].astype(out_ref.dtype)


def contract(order, g, x1, bias, weights, groups):
    rows, model = x1.shape
    depth, hidden = weights.shape[2:]
    return pl.pallas_call(
        contract_kernel,
        grid_spec=prefetched(
            (groups,),
            [
                pl.BlockSpec((rows, hidden), lambda z, order: (0, z)),
                whole(rows, model),
                whole(1, model),
            ]
            + ff_blocks(1, depth, hidden),
            whole(4, rows // 4, model),
            [pltpu.VMEM((rows, model), jnp.float32)],
        ),
        out_shape=jax.ShapeDtypeStruct((4, rows // 4, model), jnp.bfloat16),
        compiler_params=core_params(),
        cost_estimate=cost(2 * rows * model * groups * hidden, 4 * rows * groups * hidden),
        name="contract",
    )(order, g, x1, bias, *[weights] * 8)


def ff_back_kernel(order_ref, dy_ref, slope_ref, x1_ref, gain_ref, *refs):
    step = pl.program_id(0)
    near, far = joined(refs[:8])
    up_one, up_two = joined(refs[8:16])
    da_ref, ubias_ref, dx1_ref, dattn_ref, sums_ref, total_ref = refs[16:]
    rows, model = total_ref.shape
    half = model // 2

    @pl.when(step == 0)
    def _():
        total_ref[...] = jnp.zeros_like(total_ref)

    sums = None
    for first in range(0, rows, TILE):
        span = slice(first, first + TILE)
        da = into_hidden(dy_ref[span], near, far) * slope_ref[span].astype(jnp.float32)
        da = da.astype(jnp.bfloat16)
        da_ref[span] = da
        part = column_sum(da.astype(jnp.float32))
        sums = part if sums is None else sums + part
        total_ref[span, :half] += dot(da, up_one, ROWS)
        total_ref[span, half:] += dot(da, up_two, ROWS)
    ubias_ref[...] = sums

    @pl.when(step == pl.num_programs(0) - 1)
    def _():
        gains = shifts = outs = downs = jnp.zeros((1, model), jnp.float32)
        for first in range(0, rows, TILE):
            span = slice(first, first + TILE)
            normed, scale = norm_parts(x1_ref[span])
            grad = total_ref[span]
            dy = dy_ref[span].astype(jnp.float32)
            gains = gains + column_sum(grad * normed)
            shifts = shifts + column_sum(grad)
            downs = downs + column_sum(dy)
            dx1 = dy + norm_back(grad, normed, scale, gain_ref[...])
            outs = outs + column_sum(dx1)
            dx1_ref[span] = dx1
            dattn_ref[span] = dx1.astype(jnp.bfloat16)
        sums_ref[...] = jnp.concatenate([outs, gains, shifts, downs], axis=0)


def ff_back(order, dy, slope, x1, gain, weights, groups):
    rows, model = x1.shape
    depth, hidden = weights.shape[2:]
    column = pl.BlockSpec((rows, hidden), lambda z, order: (0, z))
    return pl.pallas_call(
        ff_back_kernel,
        grid_spec=prefetched(
            (groups,),
            [whole(rows, model), column, whole(rows, model), whole(1, model)]
            + ff_blocks(1, depth, hidden)
            + ff_blocks(0, depth, hidden),
            [
                column,
                pl.BlockSpec((None, 1, hidden), lambda z, order: (z, 0, 0)),
                whole(rows, model),
                whole(rows, model),
                whole(4, model),
            ],
            [pltpu.VMEM((rows, model), jnp.float32)],
        ),
        out_shape=[
            jax.ShapeDtypeStruct((rows, groups * hidden), jnp.bfloat16),
            jax.ShapeDtypeStruct((groups, 1, hidden), jnp.float32),
            jax.ShapeDtypeStruct((rows, model), jnp.float32),
            jax.ShapeDtypeStruct((rows, model), jnp.bfloat16),
            jax.ShapeDtypeStruct((4, model), jnp.float32),
        ],
        compiler_params=core_params(60),
        cost_estimate=cost(4 * rows * model * groups * hidden, 8 * rows * groups * hidden),
        name="ff_back",
    )(order, dy, slope, x1, gain, *[weights] * 16)


def mix_back_kernel(dattn_ref, near_ref, far_ref, out_ref):
    near, far = flat(near_ref), flat(far_ref)
    out_ref[...] = into_hidden(dattn_ref[...], near, far).astype(jnp.bfloat16)


def mix_back(dattn, near, far, width):
    rows, model = dattn.shape
    groups = near.shape[1]
    return pl.pallas_call(
        mix_back_kernel,
        grid=(groups,),
        in_specs=[whole(rows, model)] + [weight_block(WEIGHT_ROWS, width, 3)] * 2,
        out_specs=pl.BlockSpec((rows, width), lambda z: (0, z)),
        out_shape=jax.ShapeDtypeStruct((rows, groups * width), jnp.bfloat16),
        compiler_params=core_params(),
        cost_estimate=cost(2 * rows * model * groups * width, 6 * rows * model),
        name="mix_back",
    )(dattn, near, far)


def project_back_kernel(
    order_ref,
    grad_ref,
    x_ref,
    dx1_ref,
    gain_ref,
    near_ref,
    far_ref,
    out_ref,
    bias_ref,
    sums_ref,
    total_ref,
):
    step = pl.program_id(0)
    rows, model = total_ref.shape
    half = model // 2
    near, far = flat(near_ref), flat(far_ref)

    @pl.when(step == 0)
    def _():
        total_ref[...] = jnp.zeros_like(total_ref)

    sums = None
    for first in range(0, rows, TILE):
        span = slice(first, first + TILE)
        grad = grad_ref[span]
        part = column_sum(grad.astype(jnp.float32))
        sums = part if sums is None else sums + part
        total_ref[span, :half] += dot(grad, near, ROWS)
        total_ref[span, half:] += dot(grad, far, ROWS)
    bias_ref[...] = sums

    @pl.when(step == pl.num_programs(0) - 1)
    def _():
        gains = shifts = jnp.zeros((1, model), jnp.float32)
        for first in range(0, rows, TILE):
            span = slice(first, first + TILE)
            normed, scale = norm_parts(x_ref[span].astype(jnp.float32))
            grad = total_ref[span]
            gains = gains + column_sum(grad * normed)
            shifts = shifts + column_sum(grad)
            total_ref[span] = dx1_ref[span] + norm_back(grad, normed, scale, gain_ref[...])
        sums_ref[...] = jnp.concatenate([gains, shifts], axis=0)
        store_absolute(order_ref, total_ref, out_ref)


def project_back(order, grad, x, dx1, gain, near, far, width):
    rows, model = x.shape
    groups = near.shape[1]
    return pl.pallas_call(
        project_back_kernel,
        grid=(groups,),
        in_specs=[
            pl.BlockSpec(memory_space=pltpu.SMEM),
            pl.BlockSpec((rows, width), lambda z: (0, z)),
            whole(rows, model),
            whole(rows, model),
            whole(1, model),
            weight_block(WEIGHT_ROWS, width, 0),
            weight_block(WEIGHT_ROWS, width, 0),
        ],
        out_specs=[
            whole(4, rows // 4, model),
            pl.BlockSpec((None, 1, width), lambda z: (z, 0, 0)),
            whole(2, model),
        ],
        out_shape=[
            jax.ShapeDtypeStruct((4, rows // 4, model), jnp.bfloat16),
            jax.ShapeDtypeStruct((groups, 1, width), jnp.float32),
            jax.ShapeDtypeStruct((2, model), jnp.float32),
        ],
        scratch_shapes=[pltpu.VMEM((rows, model), jnp.float32)],
        compiler_params=core_params(),
        cost_estimate=cost(2 * rows * model * groups * width, 8 * rows * model),
        name="project_back",
    )(order, grad, x, dx1, gain, near, far)


def swap(value, axis, bits):
    count = lax.axis_size(axis)
    return lax.ppermute(value, axis, [(index, index ^ bits) for index in range(count)])


def across_x(value):
    return swap(value, "dp", 1)


def across_y(value):
    return swap(value, "ctx", 2)


def across_core(value):
    return swap(value, "ctx", 1)


def turned(value, axis, flag):
    return jnp.where(flag == 1, jnp.flip(value, axis), value)


def one_sequence(
    tokens,
    segment_ids,
    norm1_gain,
    norm1_shift,
    w_query,
    w_key,
    w_value,
    query_bias,
    value_bias,
    w_out,
    out_bias,
    norm2_gain,
    norm2_shift,
    w_up,
    up_bias,
    w_down,
    down_bias,
    out_grad,
):
    dps, ctxs, groups = (lax.axis_size(name) for name in ALL)
    owners = dps * ctxs
    at_x = lax.axis_index("dp")
    at_ctx = lax.axis_index("ctx")
    at_z = lax.axis_index("tensor")
    at_y, at_core = at_ctx // 2, at_ctx % 2
    span, model = tokens.shape[1:]
    length = span * ctxs
    heads = query_bias.shape[0]
    width = heads * HEAD_DIM
    shard = w_query.shape[0]
    hidden = w_up.shape[1]
    shared, shared_up = query_bias.shape[1], up_bias.shape[1]

    away = jnp.array([0, 4, 2, 6, 1, 5, 3, 7], jnp.int32)
    order = jnp.concatenate(
        [away ^ (at_x * ctxs + at_ctx), jnp.arange(4, dtype=jnp.int32) ^ at_ctx, at_z[None]]
    ).astype(jnp.int32)

    def to_slots(value):
        mine = lax.dynamic_slice_in_dim(value, at_z * ctxs, ctxs, axis=0)
        return [
            lax.dynamic_index_in_dim(mine, at_ctx ^ bits, 0, keepdims=False)
            for bits in range(ctxs)
        ]

    def exchanged(slots):
        return jnp.stack([slots[0]] + [swap(slots[bits], "ctx", bits) for bits in (1, 2, 3)])

    def over_groups(pieces):
        return lax.all_gather(pieces, "tensor", axis=0, tiled=True)

    small = jnp.concatenate(
        [
            norm1_gain,
            norm1_shift,
            out_bias,
            norm2_gain,
            norm2_shift,
            down_bias,
            query_bias.reshape(-1),
            value_bias.reshape(-1),
            up_bias.reshape(-1),
        ]
    )
    used = small.shape[0]
    lanes = -(-used // (16 * 1024)) * 16 * 1024
    kept = -(-used // WIDE) * WIDE
    small = jnp.pad(small, (0, lanes - used)).reshape(-1, 1024)
    pack = jnp.concatenate([w_query, w_key, w_value, w_out.T], axis=1)
    cut = shard // 2
    pack = jnp.concatenate([pack, small], axis=0)
    lines = -(-span // 1024) * 8
    segs = jnp.pad(segment_ids, ((0, 0), (0, lines * WIDE - span))).reshape(-1, lines, WIDE)
    near, far, pieces, segs = gather_first(pack, tokens, segs, cut)
    small = jnp.stack([near[..., shard : shard + 16, :], far[..., shard : shard + 16, :]])
    small = small.reshape(2, 2, 2, groups, lanes)[..., :kept]
    pack_near, pack_far = (part.reshape((4,) + part.shape[2:]) for part in (near, far))
    segs = segs.reshape(2, 2, -1)[:, :, :span]
    segs = turned(turned(segs, 0, at_y), 1, at_core)
    weights = lax.all_gather(jnp.stack([w_up, w_down.T]), ALL, axis=0, tiled=False)

    vectors = small[:, :, :, 0, : 6 * shard].reshape(owners, 6, shard)
    vectors = vectors.transpose(1, 0, 2).reshape(6, 1, model).astype(jnp.float32)
    biases = turned(turned(turned(small, 0, at_core), 1, at_y), 2, at_x)
    biases = biases.transpose(2, 1, 0, 3, 4).reshape(owners, groups, kept)
    gain_one, shift_one, bias_out, gain_two, shift_two, bias_down = (
        vectors[index] for index in range(6)
    )

    def heads_bias(first, columns):
        part = biases[:, :, first : first + heads * columns]
        part = part.reshape(owners, groups, heads, columns).transpose(1, 2, 0, 3)
        return part.reshape(groups, 1, heads * columns * owners).astype(jnp.float32)

    first = 6 * shard
    bias_query = heads_bias(first, shared)
    bias_value = heads_bias(first + heads * shared, shared)
    bias_up = heads_bias(first + 2 * heads * shared, shared_up)
    bias_qkv = jnp.concatenate([bias_query, jnp.zeros_like(bias_query), bias_value], axis=2)

    seg_row = segs.reshape(1, 1, length)
    seg_col = segs.reshape(1, length, 1)
    head_place = (jnp.arange(groups)[:, None] ^ at_z) * heads + jnp.arange(heads)[None]
    slopes = jnp.exp2(-8.0 * (head_place.reshape(-1) + 1).astype(jnp.float32) / HEADS)

    x = order_pieces(order, pieces)
    h1, qkv = project(x, gain_one, shift_one, bias_qkv, pack_near, pack_far, 3 * width)
    grad_slots, qkv = lax.optimization_barrier((to_slots(out_grad), qkv))
    qkv = qkv.reshape(1, length, groups * 3 * width)
    mixed, log_total = attend(slopes, seg_row, seg_col, qkv, groups, heads)
    mixed = mixed.reshape(length, groups * width)
    x1, h2 = mix_out(mixed, x, bias_out, gain_two, shift_two, pack_near, pack_far, width)
    activated, gelu_slope = expand(order, h2, bias_up, weights)
    result = contract(order, activated, x1, bias_down, weights, groups)

    def away(left, right):
        return matmul_left(left[:, left.shape[1] // 2 :], right).astype(jnp.bfloat16)

    def home(left, right):
        return matmul_left(left[:, : left.shape[1] // 2], right)

    def add(here, there):
        total = here.astype(jnp.float32) + there.astype(jnp.float32)
        return total.astype(there.dtype)

    def over_xy(total, x_first, depth):
        total = total.reshape(2, 2, depth, -1)
        if x_first:
            total = add(total[:, 0], across_x(total[:, 1]))
            return add(total[0], across_y(total[1]))
        total = add(total[0], across_y(total[1]))
        return add(total[0], across_x(total[1]))

    def over_z(*totals):
        widths = [total.shape[1] // groups for total in totals]
        arrived = {}
        for step in range(1, groups):
            for sign in (1, -1):
                place = at_z if sign == 1 else groups - 1 - at_z
                target = jnp.minimum(groups - step + place, groups - 1)
                target = target if sign == 1 else groups - 1 - target
                pairs = [(index, index + 1) for index in range(step)]
                if sign == -1:
                    pairs = [(groups - 1 - here, groups - 1 - there) for here, there in pairs]
                for index, (total, columns) in enumerate(zip(totals, widths)):
                    part = lax.dynamic_slice_in_dim(
                        total, (target ^ at_z) * columns, columns, axis=1
                    )
                    if step > 1:
                        part = add(arrived[index, sign], part)
                    arrived[index, sign] = lax.ppermute(part, "tensor", pairs)
        return [
            total[:, :columns].astype(jnp.float32)
            + arrived[index, 1].astype(jnp.float32)
            + arrived[index, -1].astype(jnp.float32)
            for index, (total, columns) in enumerate(zip(totals, widths))
        ]

    dy = order_pieces(order, exchanged(grad_slots))
    dy, result, activated = lax.optimization_barrier((dy, result, activated))
    result_one = over_groups(jnp.stack([result[0], across_core(result[1])]))
    result = jnp.stack([swap(result[bits], "ctx", bits) for bits in (2, 3)])
    away_down = away(dy, activated)
    home_down = home(dy, activated).astype(jnp.bfloat16)
    dy, result, away_down, home_down = lax.optimization_barrier(
        (dy, result, away_down, home_down)
    )
    result_two = over_groups(result)
    da, grad_ubias, dx1, dattn, sums_two = ff_back(
        order, dy, gelu_slope, x1, gain_two, weights, groups
    )

    from_core = across_core(away_down)
    dattn, da, from_core = lax.optimization_barrier((dattn, da, from_core))
    down = add(home_down, from_core).reshape(2, 2, shard, -1)
    do = mix_back(dattn, pack_near, pack_far, width)
    do, down = lax.optimization_barrier((do, down))
    down_part = across_y(down[1])
    dqkv = attend_back(
        slopes,
        seg_row,
        seg_col,
        qkv,
        do.reshape(1, length, groups * width),
        log_total,
        groups,
        heads,
    ).reshape(length, groups * 3 * width)
    dqkv, down_part, result_one = lax.optimization_barrier((dqkv, down_part, result_one))
    down = add(down[0], down_part)
    down_part = across_x(down[1])
    pieces_grad, grad_bias, sums_one = project_back(
        order, dqkv, x, dx1, gain_one, pack_near, pack_far, 3 * width
    )
    pieces_grad, h2, h1, dattn = lax.optimization_barrier((pieces_grad, h2, h1, dattn))
    pieces_grad = exchanged(list(pieces_grad))
    away_up = away(h2, da)
    away_qkv = away(h1, dqkv)
    away_wout = away(dattn, mixed)
    aways = away_up, away_qkv, away_wout
    pieces_grad, result_two, aways, down_part = lax.optimization_barrier(
        (pieces_grad, result_two, aways, down_part)
    )
    tokens_one, tokens_two = over_groups(pieces_grad[:2]), over_groups(pieces_grad[2:])
    outputs = place_slots(order, result_one, result_two)
    from_core = [across_core(part) for part in aways]
    up = add(home(h2, da), from_core[0]).reshape(2, 2, shard, -1)
    qkv_sum = add(home(h1, dqkv), from_core[1]).reshape(2, 2, shard, -1)
    wout_sum = add(home(dattn, mixed), from_core[2]).reshape(2, 2, shard, -1)
    down = add(down[0], down_part)
    up, qkv_sum, wout_sum, down = lax.optimization_barrier((up, qkv_sum, wout_sum, down))
    moved = across_x(up[:, 1]), across_y(qkv_sum[1]), across_y(wout_sum[1])
    (sum_down,) = over_z(down)
    sum_down = sum_down.T
    moved, sum_down = lax.optimization_barrier((moved, sum_down))
    up, qkv_sum, wout_sum = (
        add(up[:, 0], moved[0]),
        add(qkv_sum[0], moved[1]),
        add(wout_sum[0], moved[2]),
    )
    moved = across_y(up[1]), across_x(qkv_sum[1]), across_x(wout_sum[1])
    sum_up, sum_qkv, sum_wout = over_z(
        add(up[0], moved[0]), add(qkv_sum[0], moved[1]), add(wout_sum[0], moved[2])
    )
    sum_wout = sum_wout.T

    grad_vectors = jnp.concatenate([sums_one, sums_two], axis=0)
    grad_vectors = grad_vectors.reshape(6, owners, shard).transpose(1, 0, 2)
    grad_vectors = grad_vectors.reshape(owners, 1, 6 * shard)
    grad_vectors = jnp.broadcast_to(grad_vectors, (owners, groups, 6 * shard))

    def owner_bias(value, columns):
        value = value.reshape(groups, heads, 2, 2, 2, columns).transpose(4, 3, 2, 0, 1, 5)
        value = turned(turned(turned(value, 0, at_core), 1, at_y), 2, at_x)
        return value.reshape(owners, groups, heads * columns)

    grad_bias = grad_bias.reshape(groups, 3, heads, HEAD_DIM)
    grad_small = jnp.concatenate(
        [
            grad_vectors,
            owner_bias(grad_bias[:, 0], shared),
            owner_bias(grad_bias[:, 2], shared),
            owner_bias(grad_ubias, shared_up),
            jnp.zeros((owners, groups, kept - used), jnp.float32),
        ],
        axis=2,
    )
    grad_small = grad_small.reshape(owners, groups * kept)
    grad_small, sum_down = lax.optimization_barrier((grad_small, sum_down))
    small_sum = add(grad_small[:4], across_core(grad_small[4:]))
    sum_small = over_z(over_xy(small_sum, True, 1))[0].reshape(-1)
    tokens_one, tokens_two, sum_up, sum_qkv, sum_wout, sum_small = lax.optimization_barrier(
        (tokens_one, tokens_two, sum_up, sum_qkv, sum_wout, sum_small)
    )
    tokens_grad = place_slots(order, tokens_one, tokens_two)
    sums = sum_small[: 6 * shard].reshape(6, shard)
    sum_biases = sum_small[6 * shard :]
    count = heads * shared
    return (
        outputs,
        tokens_grad,
        sums[0],
        sums[1],
        sum_qkv[:, :width],
        sum_qkv[:, width : 2 * width],
        sum_qkv[:, 2 * width :],
        sum_biases[:count].reshape(heads, shared),
        sum_biases[count : 2 * count].reshape(heads, shared),
        sum_wout,
        sums[2],
        sums[3],
        sums[4],
        sum_up,
        sum_biases[2 * count : 2 * count + heads * shared_up].reshape(heads, shared_up),
        sum_down,
        sums[5],
    )


def choose_plan(tokens, *others):
    sizes = tuple(lax.axis_size(name) for name in ALL)
    if sizes == (2, 4, 4) and tokens.shape[0] == 16 and tokens.shape[1] % TILE == 0:
        return one_sequence(tokens, *others)
    return shards(tokens, *others)


def solution(mesh):
    return jax.shard_map(
        choose_plan,
        mesh=mesh,
        in_specs=(
            P("dp", "ctx", None),
            P("dp", "ctx"),
            P(("dp", "ctx")),
            P(("dp", "ctx")),
            P(("dp", "ctx"), "tensor"),
            P(("dp", "ctx"), "tensor"),
            P(("dp", "ctx"), "tensor"),
            P("tensor", ("dp", "ctx")),
            P("tensor", ("dp", "ctx")),
            P("tensor", ("dp", "ctx")),
            P(("dp", "ctx")),
            P(("dp", "ctx")),
            P(("dp", "ctx")),
            P(("dp", "ctx"), "tensor"),
            P("tensor", ("dp", "ctx")),
            P("tensor", ("dp", "ctx")),
            P(("dp", "ctx")),
            P("dp", "ctx", None),
        ),
        out_specs=(
            P("dp", "ctx", None),
            P("dp", "ctx", None),
            P(("dp", "ctx")),
            P(("dp", "ctx")),
            P(("dp", "ctx"), "tensor"),
            P(("dp", "ctx"), "tensor"),
            P(("dp", "ctx"), "tensor"),
            P("tensor", ("dp", "ctx")),
            P("tensor", ("dp", "ctx")),
            P("tensor", ("dp", "ctx")),
            P(("dp", "ctx")),
            P(("dp", "ctx")),
            P(("dp", "ctx")),
            P(("dp", "ctx"), "tensor"),
            P("tensor", ("dp", "ctx")),
            P("tensor", ("dp", "ctx")),
            P(("dp", "ctx")),
        ),
        check_vma=False,
    )
```
